128 devices in a mesh: wide: 32 (over z, y, core), narrow: 4 (over x).
Axes of the slice: x: 4, y: 4, z: 4, core: 2. Of those that a mesh axis runs over, the one named last changes fastest.
Arguments:
- psi_val: bfloat16 [128, 32768], replicated, may hold values from -6 to 6
- psi_cond: bfloat16 [32, 32768], replicated, may hold values from -6 to 6
- energy_val: float32 [128], replicated, may hold values from -8 to -1
- energy_cond: float32 [32], replicated, may hold values from 0.5 to 6
- pair_table: int32 [2048, 2], P(('wide', 'narrow')), may hold values from 0 to 127, as said below
- sphere_map: int32 [8192], replicated, may hold values from 0 to 32767, as said below
Outputs:
- chi_real: float32 [8192, 8192], P('wide', 'narrow')
- chi_imag: float32 [8192, 8192], P('wide', 'narrow')
The draws below stay inside these ranges and needn't reach their ends.
Inputs may be any that keep to these rules, and one draw needn't show every extreme that they name: `pair_table`: every row is a distinct pair; the column-1 entries are below 32; the valence bands present are 64 distinct bands, each paired with all 32 conduction bands, and band 128 - 1 is among them. `sphere_map`: distinct grid indices of the 8192 G-vectors with the smallest lengths (wrapped frequencies), in no particular order; ties among equal lengths are drawn.
All inputs are finite; a program needn't handle non-finite values.
Results may differ from the reference program's by a relative error of at most 0.004.
Values may be sent and summed in bfloat16 or wider, within the bound.
A program may use at most 128 MiB of HBM per device.

```python
import math
import jax
import jax.numpy as jnp
from jax import lax

NG = 8192
FS = 32
NVAL = 128
NC = 32
VB = 64


def draw_pair_table(key, part):
    key = jax.random.fold_in(key, 23)
    first_key, second_key = jax.random.split(key)
    shuffled = jax.random.permutation(first_key, NVAL - 1).astype(jnp.int32)
    chosen = jnp.concatenate([shuffled[:VB - 1], jnp.full((1,), NVAL - 1, jnp.int32)])
    index = jnp.arange(VB * NC, dtype=jnp.int32)
    table = jnp.stack([chosen[index // NC], index % NC], axis=1)
    order = jax.random.permutation(second_key, VB * NC)
    return table[order].astype(jnp.int32)


def draw_sphere_map(key, part):
    key = jax.random.fold_in(key, 11)
    first_key, second_key = jax.random.split(key)
    points = FS * FS * FS
    index = jnp.arange(points, dtype=jnp.int32)
    coord_x = index // (FS * FS)
    coord_y = index // FS % FS
    coord_z = index % FS
    wrap_x = jnp.where(coord_x >= FS // 2, coord_x - FS, coord_x)
    wrap_y = jnp.where(coord_y >= FS // 2, coord_y - FS, coord_y)
    wrap_z = jnp.where(coord_z >= FS // 2, coord_z - FS, coord_z)
    length_sq = wrap_x * wrap_x + wrap_y * wrap_y + wrap_z * wrap_z
    jitter = jax.random.randint(first_key, (points,), 0, 16, dtype=jnp.int32)
    scores = (length_sq * 16 + jitter) * points + index
    chosen = jnp.argsort(scores)[:NG].astype(jnp.int32)
    order = jax.random.permutation(second_key, NG)
    return chosen[order].astype(jnp.int32)


def gaussian(stream_key, dims, width, most, held_as=jnp.bfloat16):
    return jnp.clip(width * jax.random.normal(stream_key, dims, jnp.float32), -most, most).astype(held_as)


def setup_inputs(seed: int = 0) -> dict:
    key_of = jax.random.split(jax.random.key(seed), 7)
    psi_val = gaussian(key_of[0], (NVAL, FS * FS * FS), 1.0, 6.0)
    psi_cond = gaussian(key_of[1], (NC, FS * FS * FS), 1.0, 6.0)
    energy_val = jnp.clip(jax.random.uniform(key_of[2], (NVAL,), jnp.float32, -8.0, -1.0), -8.0, -1.0)
    energy_cond = jnp.clip(jax.random.uniform(key_of[3], (NC,), jnp.float32, 0.5, 6.0), 0.5, 6.0)
    pair_table = draw_pair_table(jax.random.fold_in(key_of[6], 71), 0)
    sphere_map = draw_sphere_map(jax.random.fold_in(key_of[6], 71), 0)
    return {"psi_val": psi_val, "psi_cond": psi_cond, "energy_val": energy_val, "energy_cond": energy_cond, "pair_table": pair_table, "sphere_map": sphere_map}


def reference(psi_val, psi_cond, energy_val, energy_cond, pair_table, sphere_map):

    def transform_block(pair_block):
        val_index = pair_block[:, 0]
        cond_index = pair_block[:, 1]
        density = psi_val[val_index].astype(jnp.float32) * psi_cond[cond_index].astype(jnp.float32)
        spectra = jnp.fft.fftn(density.reshape(-1, FS, FS, FS), axes=(1, 2, 3), norm='ortho')
        spectra = spectra.reshape(-1, FS * FS * FS)[:, sphere_map]
        parts = jnp.stack([jnp.real(spectra), jnp.imag(spectra)]).astype(jnp.float32)
        weight = 2.0 / ((energy_val[val_index] - energy_cond[cond_index]) * math.sqrt(VB * NC))
        return (parts.astype(jnp.bfloat16), (weight[None, :, None] * parts).astype(jnp.bfloat16))
    plain, weighted = lax.map(transform_block, pair_table.reshape(-1, 64, 2))
    plain = jnp.transpose(plain, (1, 0, 2, 3)).reshape(2, -1, NG)
    weighted = jnp.transpose(weighted, (1, 0, 2, 3)).reshape(2, -1, NG)
    columns = plain.reshape(-1, NG).astype(jnp.float32)
    left_real = weighted.reshape(-1, NG).astype(jnp.float32)
    left_imag = jnp.concatenate([weighted[1], -weighted[0]], axis=0).astype(jnp.float32)
    precise = lax.Precision.HIGHEST
    chi_real = jnp.dot(left_real.T, columns, precision=precise, preferred_element_type=jnp.float32)
    chi_imag = jnp.dot(left_imag.T, columns, precision=precise, preferred_element_type=jnp.float32)
    return (chi_real, chi_imag)
```

```python
import functools
import math

import jax
import jax.numpy as jnp
import numpy as np
from jax import lax
from jax.experimental import pallas as pl
from jax.experimental.pallas import tpu as pltpu
from jax.sharding import PartitionSpec as P

FS = 32
NC = 32
VB = 64
NG = 8192
PLANE = FS * FS
KX = 13
MESH = pl.DeviceIdType.MESH
BF = jnp.bfloat16
F32 = jnp.float32


def wrapped(index):
    return np.where(index >= FS // 2, index - FS, index)


def half_plane():
    index = np.arange(FS**3)
    length = wrapped(index // PLANE) ** 2 + wrapped(index // FS % FS) ** 2 + wrapped(index % FS) ** 2
    most = np.sort(length)[NG - 1]
    points = [
        (ky, kz)
        for ky in range(-15, 16)
        for kz in range(-15, 16)
        if ky * ky + kz * kz <= most and (ky > 0 or (ky == 0 and kz >= 0))
    ]
    points.sort(key=lambda point: (point[0] ** 2 + point[1] ** 2, point))
    return np.array(points)


POINTS = half_plane()
HALF = 256
TABLE_SCALE = 1.6211
TABLE_GAIN = 1.6245055860070914


def plane_table():
    flat = np.arange(PLANE)
    phase = (flat // FS)[:, None] * POINTS[:, 0][None, :] + (flat % FS)[:, None] * POINTS[:, 1][None, :]
    angle = (phase % FS) * (2.0 * math.pi / FS)
    table = np.zeros((PLANE, 2 * HALF), np.float64)
    table[:, : len(POINTS)] = np.cos(angle)
    table[:, HALF : HALF + len(POINTS)] = np.sin(angle)
    table[np.abs(table) < 1e-9] = 0.0
    return (table * TABLE_SCALE).astype(np.float32)


def plane_labels():
    labels = np.full((2 * HALF, 1), -1, np.int32)
    for row, (ky, kz) in enumerate(POINTS):
        labels[row, 0] = (ky % FS) * FS + kz % FS
        if (ky, kz) != (0, 0):
            labels[HALF + row, 0] = (-ky % FS) * FS + (-kz) % FS
    return labels


def cosine(step):
    return math.cos(2.0 * math.pi * step / FS)


def combine(terms):
    total = None
    for factor, term in terms:
        if abs(factor) < 1e-12:
            continue
        if abs(abs(factor) - 1.0) < 1e-12:
            value = term
            if total is None:
                total = value if factor > 0 else -value
            else:
                total = total + value if factor > 0 else total - value
        else:
            value = term * factor
            total = value if total is None else total + value
    return total


def even_part(values, period, wanted):
    half = period // 2
    stride = FS // period
    out = {}
    odd = [k for k in wanted if k % 2]
    rest = [k for k in wanted if k % 2 == 0]
    if half == 1:
        for k in wanted:
            out[k] = values[0] + values[1] if k % 2 == 0 else values[0] - values[1]
        return out
    quarter = half // 2
    if odd:
        diff = [values[j] - values[half - j] for j in range(quarter)]
        for k in odd:
            out[k] = combine([(cosine(stride * j * k), diff[j]) for j in range(quarter)])
    if rest:
        folded = [values[j] + values[half - j] for j in range(quarter)] + [values[quarter]]
        inner = even_part(folded, half, [k // 2 for k in rest])
        for k in rest:
            out[k] = inner[k // 2]
    return out


def odd_part(values, period, wanted):
    half = period // 2
    stride = FS // period
    out = {}
    odd = [k for k in wanted if k % 2]
    rest = [k for k in wanted if k % 2 == 0]
    quarter = half // 2
    if odd:
        folded = [None] + [values[j] + values[half - j] for j in range(1, quarter)] + [values[quarter]]
        for k in odd:
            out[k] = combine(
                [(math.sin(2.0 * math.pi * stride * j * k / FS), folded[j]) for j in range(1, quarter + 1)]
            )
    if rest:
        live = [k for k in rest if k % half]
        if live:
            diff = [None] + [values[j] - values[half - j] for j in range(1, quarter)]
            inner = odd_part(diff, half, [k // 2 for k in live])
            for k in live:
                out[k] = inner[k // 2]
    return out


def transform_kernel(val_ref, cond_ref, table_ref, label_ref, sphere_ref, out_ref, high, low, waves, picked):
    lanes = 128
    rows = 16

    def x_step(step, carry):
        lane = pl.multiple_of(step * lanes, lanes)
        for part in range(2):
            for block in range(NC // rows):
                density = []
                for x in range(FS):
                    cond = cond_ref[block * rows : (block + 1) * rows, pl.ds(pl.multiple_of(x * PLANE + lane, lanes), lanes)]
                    val = val_ref[part : part + 1, pl.ds(pl.multiple_of(x * PLANE + lane, lanes), lanes)]
                    density.append(cond.astype(F32) * val)
                even = [density[0]] + [density[j] + density[FS - j] for j in range(1, 16)] + [density[16]]
                odd = [None] + [density[j] - density[FS - j] for j in range(1, 16)]
                real = even_part(even, FS, list(range(KX)))
                imag = odd_part(odd, FS, list(range(KX)))
                for k in range(KX):
                    for s, value in ((0, real[k]), (1, imag.get(k))):
                        at = k * 128 + s * 64 + part * NC + block * rows
                        if value is None:
                            value = jnp.zeros((rows, lanes), F32)
                        if s == 1:
                            value = -value
                        top = value.astype(BF)
                        high[at : at + rows, pl.ds(lane, lanes)] = top
                        low[at : at + rows, pl.ds(lane, lanes)] = (value - top.astype(F32)).astype(BF)
        return carry

    lax.fori_loop(0, PLANE // lanes, x_step, 0)

    scale = FS ** (-1.5) / TABLE_GAIN

    def plane_step(k, carry):
        at = pl.multiple_of(k * 128, 128)
        both = jnp.dot(high[pl.ds(at, 128), :], table_ref[...], preferred_element_type=F32)
        both = both + jnp.dot(low[pl.ds(at, 128), :], table_ref[...], preferred_element_type=F32)
        both = both * scale
        re_cos, re_sin = both[:64, :HALF], both[:64, HALF:]
        im_cos, im_sin = both[64:, :HALF], both[64:, HALF:]
        waves[pl.ds(at, 64), :HALF] = (re_cos + im_sin).astype(BF)
        waves[pl.ds(at, 64), HALF:] = (re_cos - im_sin).astype(BF)
        waves[pl.ds(at + 64, 64), :HALF] = (im_cos - re_sin).astype(BF)
        waves[pl.ds(at + 64, 64), HALF:] = (im_cos + re_sin).astype(BF)
        return carry

    lax.fori_loop(0, KX, plane_step, 0)

    width = 256

    def pick_step(tile, carry):
        lane = pl.multiple_of(tile * width, width)
        flat = sphere_ref[:, pl.ds(lane, width)]
        kx = flat // PLANE
        ky = flat // FS % FS
        kz = flat % FS
        mirror = kx >= FS // 2
        ky = jnp.where(mirror, (FS - ky) % FS, ky)
        kz = jnp.where(mirror, (FS - kz) % FS, kz)
        kx = jnp.where(mirror, FS - kx, kx)
        sign = jnp.where(mirror, -1.0, 1.0)
        target = ky * FS + kz
        hit = jnp.where(label_ref[...] == target, 1.0, 0.0).astype(BF)
        picked[...] = jnp.dot(waves[...], hit, preferred_element_type=F32)
        total = picked[0:128, :]
        for k in range(1, KX):
            total = jnp.where(kx == k, picked[k * 128 : (k + 1) * 128, :], total)
        out_ref[0:64, pl.ds(lane, width)] = total[:64].astype(BF)
        out_ref[64:128, pl.ds(lane, width)] = (total[64:] * sign).astype(BF)
        return carry

    lax.fori_loop(0, 2048 // width, pick_step, 0)


def transform(val_rows, psi_cond, sphere_block):
    whole = pl.BlockSpec(memory_space=pltpu.VMEM)
    return pl.pallas_call(
        transform_kernel,
        out_shape=jax.ShapeDtypeStruct((128, 2048), BF),
        in_specs=[whole] * 5,
        out_specs=whole,
        scratch_shapes=[
            pltpu.VMEM((KX * 128, PLANE), BF),
            pltpu.VMEM((KX * 128, PLANE), BF),
            pltpu.VMEM((KX * 128, 2 * HALF), BF),
            pltpu.VMEM((KX * 128, 256), F32),
        ],
        compiler_params=pltpu.CompilerParams(vmem_limit_bytes=40 * 2**20),
        cost_estimate=pl.CostEstimate(flops=10**10, bytes_accessed=4 * 2**20, transcendentals=0),
        name="transform",
    )(
        val_rows,
        psi_cond,
        jnp.asarray(plane_table()).astype(BF),
        jnp.asarray(plane_labels()),
        sphere_block,
    )


ORDER = [
    (0, 0), (3, 0), (1, 0), (0, 3), (0, 1), (2, 0), (3, 3), (3, 1),
    (1, 3), (1, 1), (0, 2), (2, 3), (2, 1), (3, 2), (1, 2), (2, 2),
]
SLOT = {place: slot for slot, place in enumerate(ORDER)}


def gather_kernel(own_ref, weight_ref, real_ref, imag_ref, held, rows, part_sem, swap_sem, row_sem, send_sem):
    wide = lax.axis_index("wide")
    x = lax.axis_index("narrow")
    z, y, core = wide // 8, wide // 2 % 4, wide % 2
    a = jnp.where(core == 0, y, z)
    b = jnp.where(core == 0, z, y)

    def at(da, db, other=0):
        aa, bb = (a + da) % 4, (b + db) % 4
        return jnp.where(core == 0, bb * 8 + aa * 2, aa * 8 + bb * 2 + 1)

    peers = {
        "a+": (at(1, 0), x),
        "a-": (at(3, 0), x),
        "b+": (at(0, 1), x),
        "b-": (at(0, 3), x),
        "swap": (wide + 1 - 2 * core, x),
        "x+": (wide, (x + 1) % 4),
        "x-": (wide, (x + 3) % 4),
    }
    barrier = pltpu.get_barrier_semaphore()
    for peer in peers.values():
        pl.semaphore_signal(barrier, inc=1, device_id=peer, device_id_type=MESH)

    held[0, 0, 0:64, :] = own_ref[0:64, :]
    held[0, 1, 0:64, :] = own_ref[64:128, :]
    pl.semaphore_wait(barrier, len(peers))

    sends = []

    def view(slot, part, which=0):
        if part is None:
            return held.at[slot, :, which * 64 : which * 64 + 64, :]
        return held.at[slot, part, which * 64 : which * 64 + 64, :]

    def push(slot, part, peer, target):
        copy = pltpu.make_async_remote_copy(
            src_ref=view(slot, part),
            dst_ref=view(target, part),
            send_sem=send_sem.at[len(sends)],
            recv_sem=part_sem.at[target, part if part is not None else 0],
            device_id=peers[peer],
            device_id_type=MESH,
        )
        copy.start()
        sends.append(copy)

    def arrived(slot, part):
        pltpu.make_async_remote_copy(
            src_ref=view(slot, part),
            dst_ref=view(slot, part),
            send_sem=send_sem.at[0],
            recv_sem=part_sem.at[slot, part if part is not None else 0],
            device_id=peers["a+"],
            device_id_type=MESH,
        ).wait_recv()

    def swap_copy(slot, index):
        return pltpu.make_async_remote_copy(
            src_ref=view(slot, None, 0),
            dst_ref=view(slot, None, 1),
            send_sem=send_sem.at[index],
            recv_sem=swap_sem.at[slot],
            device_id=peers["swap"],
            device_id_type=MESH,
        )

    def own_event(slot):
        da, db = ORDER[slot]
        if slot and (da == 2 and db == 0 or db == 2):
            arrived(slot, 0)
            arrived(slot, 1)
        elif slot:
            arrived(slot, None)
        if db == 0:
            if da == 0:
                push(slot, None, "a+", SLOT[3, 0])
                push(slot, None, "a-", SLOT[1, 0])
            elif da == 3:
                push(slot, 0, "a+", SLOT[2, 0])
            elif da == 1:
                push(slot, 1, "a-", SLOT[2, 0])
            push(slot, None, "b+", SLOT[da, 3])
            push(slot, None, "b-", SLOT[da, 1])
        elif db == 3:
            push(slot, 0, "b+", SLOT[da, 2])
        elif db == 1:
            push(slot, 1, "b-", SLOT[da, 2])
        copy = swap_copy(slot, len(sends))
        copy.start()
        sends.append(copy)

    column = pl.multiple_of((y * 2 + core) * 256, 256)
    hops = ((x - z) % 4, (z - x) % 4)

    def row_copy(slot, which):
        return pltpu.make_async_remote_copy(
            src_ref=rows.at[slot, :, which * 64 : which * 64 + 64, :],
            dst_ref=rows.at[slot, :, which * 64 : which * 64 + 64, :],
            send_sem=row_sem.at[1, slot, which],
            recv_sem=row_sem.at[0, slot, which],
            device_id=peers["x+" if which == 0 else "x-"],
            device_id_type=MESH,
        )

    def row_event(slot, which, hop):
        @pl.when(hops[which] == hop)
        def _():
            if hop == 0:
                rows[slot, :, which * 64 : which * 64 + 64, :] = held[
                    slot, :, which * 64 : which * 64 + 64, pl.ds(column, 256)
                ]
            else:
                row_copy(slot, which).wait_recv()
            if hop < 3:
                row_copy(slot, which).start()

    width = 512

    def product(slot):
        left = rows[slot].reshape(256, 256).astype(F32).T
        left = left * weight_of(slot)
        left_real = left.astype(BF)
        left_imag = jnp.concatenate([left[:, 128:], -left[:, :128]], axis=1).astype(BF)

        def tile(step, carry):
            lane = pl.multiple_of(step * width, width)
            right = held[slot, :, :, pl.ds(lane, width)].reshape(256, width)
            real = jnp.dot(left_real, right, preferred_element_type=F32)
            imag = jnp.dot(left_imag, right, preferred_element_type=F32)
            if slot == 0:
                real_ref[:, pl.ds(lane, width)] = real
                imag_ref[:, pl.ds(lane, width)] = imag
            else:
                real_ref[:, pl.ds(lane, width)] += real
                imag_ref[:, pl.ds(lane, width)] += imag
            return carry

        lax.fori_loop(0, 2048 // width, tile, 0)

    def weight_of(slot):
        da, db = ORDER[slot]
        first = at(da, db)
        aa, bb = (b + da) % 4, (a + db) % 4
        second = jnp.where(core == 0, aa * 8 + bb * 2 + 1, bb * 8 + aa * 2)
        return weight_ref[first] + weight_ref[second + 32]

    lag = 6
    for event in range(16 + lag):
        if event < 16:
            own_event(event)
        if 0 <= event - 1 < 16:
            pltpu.make_async_remote_copy(
                src_ref=view(event - 1, None, 0),
                dst_ref=view(event - 1, None, 1),
                send_sem=send_sem.at[0],
                recv_sem=swap_sem.at[event - 1],
                device_id=peers["swap"],
                device_id_type=MESH,
            ).wait_recv()
        for which in range(2):
            for hop in range(4):
                slot = event - 1 - hop
                if 0 <= slot < 16:
                    row_event(slot, which, hop)
        if 0 <= event - lag + 1 < 16:
            product(event - lag + 1)

    for copy in sends:
        copy.wait_send()
    for slot in range(16):
        for which in range(2):

            @pl.when(hops[which] < 3)
            def _():
                row_copy(slot, which).wait_send()


def gather_and_multiply(own, weights):
    whole = pl.BlockSpec(memory_space=pltpu.VMEM)
    return pl.pallas_call(
        gather_kernel,
        out_shape=[jax.ShapeDtypeStruct((256, 2048), F32)] * 2,
        in_specs=[whole] * 2,
        out_specs=[whole] * 2,
        scratch_shapes=[
            pltpu.VMEM((16, 2, 128, 2048), BF),
            pltpu.VMEM((16, 2, 128, 256), BF),
            pltpu.SemaphoreType.DMA((16, 2)),
            pltpu.SemaphoreType.DMA((16,)),
            pltpu.SemaphoreType.DMA((2, 16, 2)),
            pltpu.SemaphoreType.DMA((64,)),
        ],
        compiler_params=pltpu.CompilerParams(
            collective_id=0, has_side_effects=True, vmem_limit_bytes=48 * 2**20
        ),
        cost_estimate=pl.CostEstimate(flops=2 * 4096 * 512 * 2048, bytes_accessed=8 * 2**20, transcendentals=0),
        name="gather_and_multiply",
    )(own, weights)


def on_device(psi_val, psi_cond, energy_val, energy_cond, pair_table, sphere_map):
    wide = lax.axis_index("wide")
    bands = jnp.arange(128, dtype=jnp.int32)
    present = jnp.max((pair_table[:, :1] == bands[None, :]).astype(F32), axis=0)
    present = lax.psum(present, ("wide", "narrow")) > 0.5
    rank = jnp.sum(((bands[:, None] < bands[None, :]) & present[:, None]).astype(jnp.int32), axis=0)
    chosen = present[None, :] & (rank[None, :] == jnp.arange(VB, dtype=jnp.int32)[:, None])
    band_of = jnp.sum(jnp.where(chosen, bands[None, :], 0), axis=1)
    energy_of = jnp.sum(jnp.where(chosen, energy_val[None, :], 0.0), axis=1)
    weight = 2.0 / ((energy_of[:, None] - energy_cond[None, :]) * math.sqrt(VB * NC))
    weight = weight.reshape(32, 64)
    blank = jnp.zeros_like(weight)
    first = jnp.concatenate([weight, blank, weight, blank], axis=1)
    second = jnp.concatenate([blank, weight, blank, weight], axis=1)
    weights = jnp.concatenate([first, second], axis=0).reshape(64, 1, 256)
    mine = lax.dynamic_slice(band_of, (2 * wide,), (2,))
    val_rows = jnp.concatenate(
        [lax.dynamic_slice(psi_val, (mine[i], 0), (1, psi_val.shape[1])) for i in range(2)], axis=0
    ).astype(F32)
    sphere_block = lax.dynamic_slice(sphere_map, (lax.axis_index("narrow") * 2048,), (2048,)).reshape(1, 2048)
    own = transform(val_rows, psi_cond, sphere_block)
    chi_real, chi_imag = gather_and_multiply(own, weights)
    return (chi_real, chi_imag)


def solution(mesh):
    placed = (P(), P(), P(), P(), P(("wide", "narrow"), None), P())
    return jax.shard_map(
        on_device,
        mesh=mesh,
        in_specs=placed,
        out_specs=(P("wide", "narrow"), P("wide", "narrow")),
        check_vma=False,
    )
```

```python
import math

import jax
import jax.numpy as jnp
import numpy as np
from jax import lax
from jax.experimental import pallas as pl
from jax.experimental.pallas import tpu as pltpu
from jax.sharding import PartitionSpec as P

FS = 32
NC = 32
VB = 64
NG = 8192
PLANE = FS * FS
KX = 13
MESH = pl.DeviceIdType.MESH
BF = jnp.bfloat16
F32 = jnp.float32


def wrapped(index):
    return np.where(index >= FS // 2, index - FS, index)


def half_plane():
    index = np.arange(FS**3)
    length = wrapped(index // PLANE) ** 2 + wrapped(index // FS % FS) ** 2 + wrapped(index % FS) ** 2
    most = np.sort(length)[NG - 1]
    points = [
        (ky, kz)
        for ky in range(-15, 16)
        for kz in range(-15, 16)
        if ky * ky + kz * kz <= most and (ky > 0 or (ky == 0 and kz >= 0))
    ]
    points.sort(key=lambda point: (point[0] ** 2 + point[1] ** 2, point))
    return np.array(points)


POINTS = half_plane()
HALF = 256
TABLE_SCALE = 1.6211
TABLE_GAIN = 1.6245055860070914


def plane_table():
    flat = np.arange(PLANE)
    phase = (flat // FS)[:, None] * POINTS[:, 0][None, :] + (flat % FS)[:, None] * POINTS[:, 1][None, :]
    angle = (phase % FS) * (2.0 * math.pi / FS)
    table = np.zeros((PLANE, 2 * HALF), np.float64)
    table[:, : len(POINTS)] = np.cos(angle)
    table[:, HALF : HALF + len(POINTS)] = np.sin(angle)
    table[np.abs(table) < 1e-9] = 0.0
    return (table * TABLE_SCALE).astype(np.float32)


def plane_labels():
    labels = np.full((2 * HALF, 1), -1, np.int32)
    for row, (ky, kz) in enumerate(POINTS):
        labels[row, 0] = (ky % FS) * FS + kz % FS
        if (ky, kz) != (0, 0):
            labels[HALF + row, 0] = (-ky % FS) * FS + (-kz) % FS
    return labels


def cosine(step):
    return math.cos(2.0 * math.pi * step / FS)


def combine(terms):
    total = None
    for factor, term in terms:
        if abs(factor) < 1e-12:
            continue
        if abs(abs(factor) - 1.0) < 1e-12:
            value = term
            if total is None:
                total = value if factor > 0 else -value
            else:
                total = total + value if factor > 0 else total - value
        else:
            value = term * factor
            total = value if total is None else total + value
    return total


def even_part(values, period, wanted):
    half = period // 2
    stride = FS // period
    out = {}
    odd = [k for k in wanted if k % 2]
    rest = [k for k in wanted if k % 2 == 0]
    if half == 1:
        for k in wanted:
            out[k] = values[0] + values[1] if k % 2 == 0 else values[0] - values[1]
        return out
    quarter = half // 2
    if odd:
        diff = [values[j] - values[half - j] for j in range(quarter)]
        for k in odd:
            out[k] = combine([(cosine(stride * j * k), diff[j]) for j in range(quarter)])
    if rest:
        folded = [values[j] + values[half - j] for j in range(quarter)] + [values[quarter]]
        inner = even_part(folded, half, [k // 2 for k in rest])
        for k in rest:
            out[k] = inner[k // 2]
    return out


def odd_part(values, period, wanted):
    half = period // 2
    stride = FS // period
    out = {}
    odd = [k for k in wanted if k % 2]
    rest = [k for k in wanted if k % 2 == 0]
    quarter = half // 2
    if odd:
        folded = [None] + [values[j] + values[half - j] for j in range(1, quarter)] + [values[quarter]]
        for k in odd:
            out[k] = combine(
                [(math.sin(2.0 * math.pi * stride * j * k / FS), folded[j]) for j in range(1, quarter + 1)]
            )
    if rest:
        live = [k for k in rest if k % half]
        if live:
            diff = [None] + [values[j] - values[half - j] for j in range(1, quarter)]
            inner = odd_part(diff, half, [k // 2 for k in live])
            for k in live:
                out[k] = inner[k // 2]
    return out


def exchange(mask, groups, own, got, out_sem, in_sem):
    own[0] = mask
    done, count = [], 0
    for step, group in enumerate(groups):
        copies = []
        for peer in group:
            copy = pltpu.make_async_remote_copy(
                src_ref=own.at[step],
                dst_ref=got.at[count],
                send_sem=out_sem.at[count],
                recv_sem=in_sem.at[count],
                device_id=peer,
                device_id_type=MESH,
            )
            copy.start()
            copies.append((copy, count))
            count += 1
        total = own[step]
        for copy, at in copies:
            copy.wait_recv()
            total = jnp.maximum(total, got[at])
        own[step + 1] = total
        done += copies
    for copy, _ in done:
        copy.wait_send()
    return own[len(groups)][0:1, :]


def deal(present, wide, val_energy, cond_energy, weight_ref):
    band = lax.broadcasted_iota(jnp.int32, (128, 128), 0)
    other = lax.broadcasted_iota(jnp.int32, (128, 128), 1)
    rank = jnp.sum(jnp.where(other < band, present, 0), axis=1, keepdims=True)
    across = jnp.sum(jnp.where(other == band, rank, 0), axis=0, keepdims=True)
    across = jnp.where(present > 0, across, -1)
    device = lax.broadcasted_iota(jnp.int32, (32, 128), 0)
    energy = [jnp.sum(jnp.where(across == 2 * device + i, val_energy, 0.0), axis=1, keepdims=True) for i in range(2)]
    lane = lax.broadcasted_iota(jnp.int32, (32, 256), 1)
    cond = jnp.concatenate([cond_energy] * 8, axis=1)
    gap = jnp.where(lane // NC % 2 == 0, energy[0], energy[1]) - cond
    weight_ref[...] = 2.0 / (gap * math.sqrt(VB * NC))
    row = lax.broadcasted_iota(jnp.int32, (8, 128), 0)
    return jnp.where((across == 2 * wide + row) & (row < 2), 1.0, 0.0).astype(BF)


def pick_rows(psi_ref, chosen, row_ref):
    def step(x, carry):
        lane = pl.multiple_of(x * PLANE, PLANE)
        row_ref[:, pl.ds(lane, PLANE)] = jnp.dot(chosen, psi_ref[:, pl.ds(lane, PLANE)], preferred_element_type=F32)
        return carry

    lax.fori_loop(0, FS, step, 0)


def transform(val_ref, cond_ref, table_ref, label_ref, sphere_ref, first_column, store, high, low, waves, picked):
    lanes = 128
    rows = 16

    def x_step(step, carry):
        lane = pl.multiple_of(step * lanes, lanes)
        for part in range(2):
            for block in range(NC // rows):
                density = []
                for x in range(FS):
                    cond = cond_ref[block * rows : (block + 1) * rows, pl.ds(pl.multiple_of(x * PLANE + lane, lanes), lanes)]
                    val = val_ref[part : part + 1, pl.ds(pl.multiple_of(x * PLANE + lane, lanes), lanes)]
                    density.append(cond.astype(F32) * val)
                even = [density[0]] + [density[j] + density[FS - j] for j in range(1, 16)] + [density[16]]
                odd = [None] + [density[j] - density[FS - j] for j in range(1, 16)]
                real = even_part(even, FS, list(range(KX)))
                imag = odd_part(odd, FS, list(range(KX)))
                for k in range(KX):
                    for s, value in ((0, real[k]), (1, imag.get(k))):
                        at = k * 128 + s * 64 + part * NC + block * rows
                        if value is None:
                            value = jnp.zeros((rows, lanes), F32)
                        if s == 1:
                            value = -value
                        top = value.astype(BF)
                        high[at : at + rows, pl.ds(lane, lanes)] = top
                        low[at : at + rows, pl.ds(lane, lanes)] = (value - top.astype(F32)).astype(BF)
        return carry

    lax.fori_loop(0, PLANE // lanes, x_step, 0)

    scale = FS ** (-1.5) / TABLE_GAIN

    def plane_step(k, carry):
        at = pl.multiple_of(k * 128, 128)
        both = jnp.dot(high[pl.ds(at, 128), :], table_ref[...], preferred_element_type=F32)
        both = both + jnp.dot(low[pl.ds(at, 128), :], table_ref[...], preferred_element_type=F32)
        both = both * scale
        re_cos, re_sin = both[:64, :HALF], both[:64, HALF:]
        im_cos, im_sin = both[64:, :HALF], both[64:, HALF:]
        waves[pl.ds(at, 64), :HALF] = (re_cos + im_sin).astype(BF)
        waves[pl.ds(at, 64), HALF:] = (re_cos - im_sin).astype(BF)
        waves[pl.ds(at + 64, 64), :HALF] = (im_cos - re_sin).astype(BF)
        waves[pl.ds(at + 64, 64), HALF:] = (im_cos + re_sin).astype(BF)
        return carry

    lax.fori_loop(0, KX, plane_step, 0)

    width = 256

    def pick_step(tile, carry):
        lane = pl.multiple_of(tile * width, width)
        flat = sphere_ref[:, pl.ds(pl.multiple_of(first_column + lane, width), width)]
        kx = flat // PLANE
        ky = flat // FS % FS
        kz = flat % FS
        mirror = kx >= FS // 2
        ky = jnp.where(mirror, (FS - ky) % FS, ky)
        kz = jnp.where(mirror, (FS - kz) % FS, kz)
        kx = jnp.where(mirror, FS - kx, kx)
        sign = jnp.where(mirror, -1.0, 1.0)
        target = ky * FS + kz
        hit = jnp.where(label_ref[...] == target, 1.0, 0.0).astype(BF)
        picked[...] = jnp.dot(waves[...], hit, preferred_element_type=F32)
        total = picked[0:128, :]
        for k in range(1, KX):
            total = jnp.where(kx == k, picked[k * 128 : (k + 1) * 128, :], total)
        store(lane, width, total[:64].astype(BF), (total[64:] * sign).astype(BF))
        return carry

    lax.fori_loop(0, 2048 // width, pick_step, 0)


ORDER = [
    (0, 0), (3, 0), (1, 0), (0, 3), (0, 1), (2, 0), (3, 3), (3, 1),
    (1, 3), (1, 1), (0, 2), (2, 3), (2, 1), (3, 2), (1, 2), (2, 2),
]
SLOT = {place: slot for slot, place in enumerate(ORDER)}


def whole_kernel(
    table_ref, val_energy, cond_energy, sphere_ref, label_ref, psi_val, psi_cond, plane_ref, real_ref, imag_ref,
    held, rows, val_all, cond_all, plane, val_rows, high, low, waves, picked, weight_ref, own_mask, got_mask,
    load_sem, out_sem, in_sem, part_sem, swap_sem, row_sem, send_sem,
):
    wide = lax.axis_index("wide")
    x = lax.axis_index("narrow")
    z, y, core = wide // 8, wide // 2 % 4, wide % 2
    a = jnp.where(core == 0, y, z)
    b = jnp.where(core == 0, z, y)

    def at(da, db, other=0):
        aa, bb = (a + da) % 4, (b + db) % 4
        return jnp.where(core == 0, bb * 8 + aa * 2, aa * 8 + bb * 2 + 1)

    peers = {
        "a+": (at(1, 0), x),
        "a-": (at(3, 0), x),
        "b+": (at(0, 1), x),
        "b-": (at(0, 3), x),
        "swap": (wide + 1 - 2 * core, x),
        "x+": (wide, (x + 1) % 4),
        "x-": (wide, (x + 3) % 4),
    }
    def line(dz, dy):
        return ((z + dz) % 4 * 8 + (y + dy) % 4 * 2 + core, x)

    ring = [(wide, (x + d) % 4) for d in (1, 2, 3)]
    twin = wide + 1 - 2 * core
    near = ring + [(twin, x)] + [(twin, (x + d) % 4) for d in (1, 2, 3)]
    far = [line(dz, dy) for dz in range(4) for dy in range(4) if dz or dy]
    barrier = pltpu.get_barrier_semaphore()
    for peer in near + far:
        pl.semaphore_signal(barrier, inc=1, device_id=peer, device_id_type=MESH)
    loads = [
        pltpu.make_async_copy(source, target, load_sem.at[i])
        for i, (source, target) in enumerate(((psi_val, val_all), (psi_cond, cond_all), (plane_ref, plane)))
    ]
    for load in loads:
        load.start()

    band = lax.broadcasted_iota(jnp.int32, (128, 16), 0)
    there = jnp.max(jnp.where(band == table_ref[0:1, :], 1, 0), axis=1, keepdims=True)
    diagonal = lax.broadcasted_iota(jnp.int32, (128, 128), 0) == lax.broadcasted_iota(jnp.int32, (128, 128), 1)
    mask = jnp.broadcast_to(jnp.max(jnp.where(diagonal, there, 0), axis=0, keepdims=True), (8, 128))
    pl.semaphore_wait(barrier, len(near) + len(far))
    present = exchange(mask, (near, far), own_mask, got_mask, out_sem, in_sem)
    mine = deal(present, wide, val_energy[...], cond_energy[...], weight_ref)

    for load in loads:
        load.wait()
    pick_rows(val_all, mine, val_rows)

    def store(lane, width, real, imag):
        held[0, 0, 0:64, pl.ds(lane, width)] = real
        held[0, 1, 0:64, pl.ds(lane, width)] = imag

    transform(val_rows, cond_all, plane, label_ref, sphere_ref, x * 2048, store, high, low, waves, picked)

    sends = []

    def view(slot, part, which=0):
        if part is None:
            return held.at[slot, :, which * 64 : which * 64 + 64, :]
        return held.at[slot, part, which * 64 : which * 64 + 64, :]

    def push(slot, part, peer, target):
        copy = pltpu.make_async_remote_copy(
            src_ref=view(slot, part),
            dst_ref=view(target, part),
            send_sem=send_sem.at[len(sends)],
            recv_sem=part_sem.at[target, part if part is not None else 0],
            device_id=peers[peer],
            device_id_type=MESH,
        )
        copy.start()
        sends.append(copy)

    def arrived(slot, part):
        pltpu.make_async_remote_copy(
            src_ref=view(slot, part),
            dst_ref=view(slot, part),
            send_sem=send_sem.at[0],
            recv_sem=part_sem.at[slot, part if part is not None else 0],
            device_id=peers["a+"],
            device_id_type=MESH,
        ).wait_recv()

    def swap_copy(slot, index):
        return pltpu.make_async_remote_copy(
            src_ref=view(slot, None, 0),
            dst_ref=view(slot, None, 1),
            send_sem=send_sem.at[index],
            recv_sem=swap_sem.at[slot],
            device_id=peers["swap"],
            device_id_type=MESH,
        )

    def own_event(slot):
        da, db = ORDER[slot]
        if slot and (da == 2 and db == 0 or db == 2):
            arrived(slot, 0)
            arrived(slot, 1)
        elif slot:
            arrived(slot, None)
        if db == 0:
            if da == 0:
                push(slot, None, "a+", SLOT[3, 0])
                push(slot, None, "a-", SLOT[1, 0])
            elif da == 3:
                push(slot, 0, "a+", SLOT[2, 0])
            elif da == 1:
                push(slot, 1, "a-", SLOT[2, 0])
            push(slot, None, "b+", SLOT[da, 3])
            push(slot, None, "b-", SLOT[da, 1])
        elif db == 3:
            push(slot, 0, "b+", SLOT[da, 2])
        elif db == 1:
            push(slot, 1, "b-", SLOT[da, 2])
        copy = swap_copy(slot, len(sends))
        copy.start()
        sends.append(copy)

    column = pl.multiple_of((y * 2 + core) * 256, 256)
    hops = ((x - z) % 4, (z - x) % 4)

    def row_copy(slot, which):
        return pltpu.make_async_remote_copy(
            src_ref=rows.at[slot, :, which * 64 : which * 64 + 64, :],
            dst_ref=rows.at[slot, :, which * 64 : which * 64 + 64, :],
            send_sem=row_sem.at[1, slot, which],
            recv_sem=row_sem.at[0, slot, which],
            device_id=peers["x+" if which == 0 else "x-"],
            device_id_type=MESH,
        )

    def row_event(slot, which, hop):
        @pl.when(hops[which] == hop)
        def _():
            if hop == 0:
                rows[slot, :, which * 64 : which * 64 + 64, :] = held[
                    slot, :, which * 64 : which * 64 + 64, pl.ds(column, 256)
                ]
            else:
                row_copy(slot, which).wait_recv()
            if hop < 3:
                row_copy(slot, which).start()

    width = 512

    def product(slot):
        left = rows[slot].reshape(256, 256).astype(F32).T
        left = left * weight_of(slot)
        left_real = left.astype(BF)
        left_imag = jnp.concatenate([left[:, 128:], -left[:, :128]], axis=1).astype(BF)

        def tile(step, carry):
            lane = pl.multiple_of(step * width, width)
            right = held[slot, :, :, pl.ds(lane, width)].reshape(256, width)
            real = jnp.dot(left_real, right, preferred_element_type=F32)
            imag = jnp.dot(left_imag, right, preferred_element_type=F32)
            if slot == 0:
                real_ref[:, pl.ds(lane, width)] = real
                imag_ref[:, pl.ds(lane, width)] = imag
            else:
                real_ref[:, pl.ds(lane, width)] += real
                imag_ref[:, pl.ds(lane, width)] += imag
            return carry

        lax.fori_loop(0, 2048 // width, tile, 0)

    def weight_of(slot):
        da, db = ORDER[slot]
        first = at(da, db)
        aa, bb = (b + da) % 4, (a + db) % 4
        second = jnp.where(core == 0, aa * 8 + bb * 2 + 1, bb * 8 + aa * 2)
        lane = lax.broadcasted_iota(jnp.int32, (1, 256), 1)
        return jnp.where(lane // 64 % 2 == 0, weight_ref[pl.ds(first, 1), :], weight_ref[pl.ds(second, 1), :])

    lag = 6
    for event in range(16 + lag):
        if event < 16:
            own_event(event)
        if 0 <= event - 1 < 16:
            pltpu.make_async_remote_copy(
                src_ref=view(event - 1, None, 0),
                dst_ref=view(event - 1, None, 1),
                send_sem=send_sem.at[0],
                recv_sem=swap_sem.at[event - 1],
                device_id=peers["swap"],
                device_id_type=MESH,
            ).wait_recv()
        for which in range(2):
            for hop in range(4):
                slot = event - 1 - hop
                if 0 <= slot < 16:
                    row_event(slot, which, hop)
        if 0 <= event - lag + 1 < 16:
            product(event - lag + 1)

    for copy in sends:
        copy.wait_send()
    for slot in range(16):
        for which in range(2):

            @pl.when(hops[which] < 3)
            def _():
                row_copy(slot, which).wait_send()


def on_device(psi_val, psi_cond, energy_val, energy_cond, pair_table, sphere_map):
    vmem = pl.BlockSpec(memory_space=pltpu.VMEM)
    hbm = pl.BlockSpec(memory_space=pl.ANY)
    return pl.pallas_call(
        whole_kernel,
        out_shape=[jax.ShapeDtypeStruct((256, 2048), F32)] * 2,
        in_specs=[vmem] * 5 + [hbm] * 3,
        out_specs=[vmem] * 2,
        scratch_shapes=[
            pltpu.VMEM((16, 2, 128, 2048), BF),
            pltpu.VMEM((16, 2, 128, 256), BF),
            pltpu.VMEM((128, FS**3), BF),
            pltpu.VMEM((NC, FS**3), BF),
            pltpu.VMEM((PLANE, 2 * HALF), BF),
            pltpu.VMEM((8, FS**3), F32),
            pltpu.VMEM((KX * 128, PLANE), BF),
            pltpu.VMEM((KX * 128, PLANE), BF),
            pltpu.VMEM((KX * 128, 2 * HALF), BF),
            pltpu.VMEM((KX * 128, 256), F32),
            pltpu.VMEM((32, 256), F32),
            pltpu.VMEM((3, 8, 128), jnp.int32),
            pltpu.VMEM((22, 8, 128), jnp.int32),
            pltpu.SemaphoreType.DMA((3,)),
            pltpu.SemaphoreType.DMA((22,)),
            pltpu.SemaphoreType.DMA((22,)),
            pltpu.SemaphoreType.DMA((16, 2)),
            pltpu.SemaphoreType.DMA((16,)),
            pltpu.SemaphoreType.DMA((2, 16, 2)),
            pltpu.SemaphoreType.DMA((64,)),
        ],
        compiler_params=pltpu.CompilerParams(
            collective_id=0, has_side_effects=True, vmem_limit_bytes=58 * 2**20
        ),
        cost_estimate=pl.CostEstimate(flops=2 * 4096 * 512 * 2048, bytes_accessed=20 * 2**20, transcendentals=0),
        name="polarizability",
    )(
        pair_table.T,
        energy_val.reshape(1, -1),
        energy_cond.reshape(1, -1),
        sphere_map.reshape(1, -1),
        jnp.asarray(plane_labels()),
        psi_val,
        psi_cond,
        jnp.asarray(plane_table()).astype(BF),
    )


def solution(mesh):
    placed = (P(), P(), P(), P(), P(("wide", "narrow"), None), P())
    return jax.shard_map(
        on_device,
        mesh=mesh,
        in_specs=placed,
        out_specs=(P("wide", "narrow"), P("wide", "narrow")),
        check_vma=False,
    )
```

```python
import functools
import math

import jax
import jax.numpy as jnp
import numpy as np
from jax import lax
from jax.experimental import pallas as pl
from jax.experimental.pallas import tpu as pltpu
from jax.sharding import PartitionSpec as P

FS = 32
NC = 32
VB = 64
NG = 8192
PLANE = FS * FS
KX = 13
MESH = pl.DeviceIdType.MESH
BF = jnp.bfloat16
F32 = jnp.float32


def wrapped(index):
    return np.where(index >= FS // 2, index - FS, index)


def half_plane():
    index = np.arange(FS**3)
    length = wrapped(index // PLANE) ** 2 + wrapped(index // FS % FS) ** 2 + wrapped(index % FS) ** 2
    most = np.sort(length)[NG - 1]
    points = [
        (ky, kz)
        for ky in range(-15, 16)
        for kz in range(-15, 16)
        if ky * ky + kz * kz <= most and (ky > 0 or (ky == 0 and kz >= 0))
    ]
    points.sort(key=lambda point: (point[0] ** 2 + point[1] ** 2, point))
    return np.array(points)


POINTS = half_plane()
HALF = 256
TABLE_SCALE = 1.6211
TABLE_GAIN = 1.6245055860070914


NEAR = 128
FAR_KX = 9


def columns_of(first, second):
    return np.concatenate([first[:, :NEAR], second[:, :NEAR], first[:, NEAR:], second[:, NEAR:]], axis=1)


def plane_table():
    flat = np.arange(PLANE)
    phase = (flat // FS)[:, None] * POINTS[:, 0][None, :] + (flat % FS)[:, None] * POINTS[:, 1][None, :]
    angle = (phase % FS) * (2.0 * math.pi / FS)
    parts = []
    for wave in (np.cos(angle), np.sin(angle)):
        part = np.zeros((PLANE, HALF), np.float64)
        part[:, : len(POINTS)] = wave
        part[np.abs(part) < 1e-9] = 0.0
        parts.append(part)
    return (columns_of(*parts) * TABLE_SCALE).astype(np.float32)


def plane_labels():
    parts = np.full((2, HALF), -1, np.int32)
    for row, (ky, kz) in enumerate(POINTS):
        parts[0, row] = (ky % FS) * FS + kz % FS
        if (ky, kz) != (0, 0):
            parts[1, row] = (-ky % FS) * FS + (-kz) % FS
    return columns_of(parts[:1], parts[1:]).reshape(2 * HALF, 1)


def cosine(step):
    return math.cos(2.0 * math.pi * step / FS)


def combine(terms):
    total = None
    for factor, term in terms:
        if abs(factor) < 1e-12:
            continue
        if abs(abs(factor) - 1.0) < 1e-12:
            value = term
            if total is None:
                total = value if factor > 0 else -value
            else:
                total = total + value if factor > 0 else total - value
        else:
            value = term * factor
            total = value if total is None else total + value
    return total


def even_part(values, period, wanted):
    half = period // 2
    stride = FS // period
    out = {}
    odd = [k for k in wanted if k % 2]
    rest = [k for k in wanted if k % 2 == 0]
    if half == 1:
        for k in wanted:
            out[k] = values[0] + values[1] if k % 2 == 0 else values[0] - values[1]
        return out
    quarter = half // 2
    if odd:
        diff = [values[j] - values[half - j] for j in range(quarter)]
        for k in odd:
            out[k] = combine([(cosine(stride * j * k), diff[j]) for j in range(quarter)])
    if rest:
        folded = [values[j] + values[half - j] for j in range(quarter)] + [values[quarter]]
        inner = even_part(folded, half, [k // 2 for k in rest])
        for k in rest:
            out[k] = inner[k // 2]
    return out


def odd_part(values, period, wanted):
    half = period // 2
    stride = FS // period
    out = {}
    odd = [k for k in wanted if k % 2]
    rest = [k for k in wanted if k % 2 == 0]
    quarter = half // 2
    if odd:
        folded = [None] + [values[j] + values[half - j] for j in range(1, quarter)] + [values[quarter]]
        for k in odd:
            out[k] = combine(
                [(math.sin(2.0 * math.pi * stride * j * k / FS), folded[j]) for j in range(1, quarter + 1)]
            )
    if rest:
        live = [k for k in rest if k % half]
        if live:
            diff = [None] + [values[j] - values[half - j] for j in range(1, quarter)]
            inner = odd_part(diff, half, [k // 2 for k in live])
            for k in live:
                out[k] = inner[k // 2]
    return out


def exchange(mask, groups, own, got, out_sem, in_sem, work):
    own[0] = mask
    done, count = [], 0
    for step, group in enumerate(groups):
        copies = []
        for peer in group:
            copy = pltpu.make_async_remote_copy(
                src_ref=own.at[step],
                dst_ref=got.at[count],
                send_sem=out_sem.at[count],
                recv_sem=in_sem.at[count],
                device_id=peer,
                device_id_type=MESH,
            )
            copy.start()
            copies.append((copy, count))
            count += 1
        work(step)
        total = own[step]
        for copy, at in copies:
            copy.wait_recv()
            total = jnp.maximum(total, got[at])
        own[step + 1] = total
        done += copies
    for copy, _ in done:
        copy.wait_send()
    return own[len(groups)][0:1, :]


def deal(present, wide, val_energy, cond_energy, weight_ref):
    band = lax.broadcasted_iota(jnp.int32, (128, 128), 0)
    other = lax.broadcasted_iota(jnp.int32, (128, 128), 1)
    rank = jnp.sum(jnp.where(other < band, present, 0), axis=1, keepdims=True)
    across = jnp.sum(jnp.where(other == band, rank, 0), axis=0, keepdims=True)
    across = jnp.where(present > 0, across, -1)
    device = lax.broadcasted_iota(jnp.int32, (32, 128), 0)
    energy = [jnp.sum(jnp.where(across == 2 * device + i, val_energy, 0.0), axis=1, keepdims=True) for i in range(2)]
    lane = lax.broadcasted_iota(jnp.int32, (32, 256), 1)
    cond = jnp.concatenate([cond_energy] * 8, axis=1)
    gap = jnp.where(lane // NC % 2 == 0, energy[0], energy[1]) - cond
    weight_ref[...] = 2.0 / (gap * math.sqrt(VB * NC))
    row = lax.broadcasted_iota(jnp.int32, (8, 128), 0)
    return jnp.where((across == 2 * wide + row) & (row < 2), 1.0, 0.0)


def pick_rows(psi_ref, chosen, row_ref):
    blank = jnp.zeros_like(chosen[0:2])
    pad = jnp.zeros((4, 256), F32)
    both = jnp.concatenate([chosen[0:2], blank], axis=1)
    left = jnp.concatenate([both, jnp.concatenate([blank, chosen[0:2]], axis=1), pad], axis=0).astype(BF)
    half = PLANE // 2

    def step(x, carry):
        first = pl.ds(pl.multiple_of(x * PLANE, PLANE), half)
        second = pl.ds(pl.multiple_of(x * PLANE + half, half), half)
        right = jnp.concatenate([psi_ref[:, first], psi_ref[:, second]], axis=0)
        found = jnp.dot(left, right, preferred_element_type=F32)
        row_ref[0:2, first] = found[0:2]
        row_ref[0:2, second] = found[2:4]
        return carry

    lax.fori_loop(0, FS, step, 0)


WIDTH = 256


def columns_step(tile, label_ref, sphere_ref, first_column, hit, place):
    lane = pl.multiple_of(tile * WIDTH, WIDTH)
    flat = sphere_ref[:, pl.ds(pl.multiple_of(first_column + lane, WIDTH), WIDTH)]
    kx = flat // PLANE
    ky = flat // FS % FS
    kz = flat % FS
    mirror = kx >= FS // 2
    ky = jnp.where(mirror, (FS - ky) % FS, ky)
    kz = jnp.where(mirror, (FS - kz) % FS, kz)
    place[0:1, pl.ds(lane, WIDTH)] = jnp.where(mirror, FS - kx, kx)
    place[1:2, pl.ds(lane, WIDTH)] = jnp.where(mirror, -1, 1)
    target = ky * FS + kz
    hit[:, pl.ds(lane, WIDTH)] = jnp.where(label_ref[...] == target, 1.0, 0.0).astype(BF)


def transform_steps(first, count, val_ref, cond_ref, table_ref, hit, place, store, high, low, sums, waves, picked):
    lanes = 128
    rows = 16
    pair = 2 * count
    middle = FAR_KX * pair
    every = KX * pair

    def x_block(block):
        part, cond_row = (first + block * rows) // NC, (first + block * rows) % NC

        def x_step(step, carry):
            lane = pl.multiple_of(step * lanes, lanes)
            density = []
            for x in range(FS):
                at = pl.ds(pl.multiple_of(x * PLANE + lane, lanes), lanes)
                density.append(cond_ref[cond_row : cond_row + rows, at].astype(F32) * val_ref[part : part + 1, at])
            even = [density[0]] + [density[j] + density[FS - j] for j in range(1, 16)] + [density[16]]
            odd = [None] + [density[j] - density[FS - j] for j in range(1, 16)]
            real = even_part(even, FS, list(range(KX)))
            imag = odd_part(odd, FS, list(range(KX)))
            for k in range(KX):
                for s, value in ((0, real[k]), (1, imag.get(k))):
                    at = k * pair + s * count + block * rows
                    if value is None:
                        value = jnp.zeros((rows, lanes), F32)
                    if s == 1:
                        value = -value
                    top = value.astype(BF)
                    high[at : at + rows, pl.ds(lane, lanes)] = top
                    low[at : at + rows, pl.ds(lane, lanes)] = (value - top.astype(F32)).astype(BF)
            return carry

        lax.fori_loop(0, PLANE // lanes, x_step, 0)

    def plane(side):
        live = every if side == 0 else middle
        table = table_ref[:, side * HALF : (side + 1) * HALF]
        both = jnp.dot(high[0:live, :], table, preferred_element_type=F32)
        sums[0:live, :] = both + jnp.dot(low[0:live, :], table, preferred_element_type=F32)
        scale = FS ** (-1.5) / TABLE_GAIN
        left, right = side * HALF, side * HALF + NEAR

        def combine_step(k, carry):
            at = pl.multiple_of(k * pair, pair)
            re = pl.ds(at, count)
            im = pl.ds(pl.multiple_of(at + count, count), count)
            re_cos, re_sin = sums[re, :NEAR] * scale, sums[re, NEAR:] * scale
            im_cos, im_sin = sums[im, :NEAR] * scale, sums[im, NEAR:] * scale
            waves[re, left : left + NEAR] = (re_cos + im_sin).astype(BF)
            waves[re, right : right + NEAR] = (re_cos - im_sin).astype(BF)
            waves[im, left : left + NEAR] = (im_cos - re_sin).astype(BF)
            waves[im, right : right + NEAR] = (im_cos + re_sin).astype(BF)
            return carry

        lax.fori_loop(0, KX if side == 0 else FAR_KX, combine_step, 0)

    def pick(tiles):
        def pick_step(tile, carry):
            lane = pl.multiple_of(tile * WIDTH, WIDTH)
            at = pl.ds(lane, WIDTH)
            picked[0:middle, :] = jnp.dot(waves[0:middle, :], hit[:, at], preferred_element_type=F32)
            picked[middle:every, :] = jnp.dot(waves[middle:every, :HALF], hit[:HALF, at], preferred_element_type=F32)
            kx = place[0:1, at]
            total = picked[0:pair, :]
            for k in range(1, KX):
                total = jnp.where(kx == k, picked[k * pair : (k + 1) * pair, :], total)
            sign = place[1:2, at].astype(F32)
            store(lane, total[:count].astype(BF), (total[count:] * sign).astype(BF))
            return carry

        lax.fori_loop(tiles[0], tiles[1], pick_step, 0)

    steps = [functools.partial(x_block, block) for block in range(count // rows)]
    steps += [functools.partial(plane, side) for side in range(2)]
    tiles = 2048 // WIDTH
    return steps + [functools.partial(pick, (i, i + tiles // 4)) for i in range(0, tiles, tiles // 4)]


ORDER = [
    (0, 0), (3, 0), (1, 0), (0, 3), (0, 1), (2, 0), (3, 3), (3, 1),
    (1, 3), (1, 1), (0, 2), (2, 3), (2, 1), (3, 2), (1, 2), (2, 2),
]
SLOT = {place: slot for slot, place in enumerate(ORDER)}
COLORS = [(0, 64)]
SIZES = [last - first for first, last in COLORS]
MOST = max(SIZES)


def groups_of(size):
    count = max(1, 256 // (2 * size))
    return [(slot, min(slot + count, 16)) for slot in range(0, 16, count)]


def moves(slot):
    da, db = ORDER[slot]
    out = []
    if db == 0:
        if da == 0:
            out += [(None, "a+", SLOT[3, 0]), (None, "a-", SLOT[1, 0])]
        elif da == 3:
            out += [(0, "a+", SLOT[2, 0])]
        elif da == 1:
            out += [(1, "a-", SLOT[2, 0])]
        out += [(None, "b+", SLOT[da, 3]), (None, "b-", SLOT[da, 1])]
    elif db == 3:
        out += [(0, "b+", SLOT[da, 2])]
    elif db == 1:
        out += [(1, "b-", SLOT[da, 2])]
    return out


def in_halves(slot):
    da, db = ORDER[slot]
    return (da == 2 and db == 0) or db == 2


WAVES = [[0], [1, 2, 3, 4], [5, 6, 7], [8, 9, 10], [11, 12], [13, 14], [15]]
LATE = 11


def order_of_work():
    turns = [(color, wave) for wave in range(1, len(WAVES)) for color in range(len(COLORS))]
    turns = [(color, 0) for color in range(len(COLORS))] + turns
    order, left = [], {}
    for color, size in enumerate(SIZES):
        for group, (first, last) in enumerate(groups_of(size)):
            left[color, group] = set(range(first, last))
    for turn in range(len(turns) + 3):
        if turn < len(turns):
            color, wave = turns[turn]
            if wave == 0:
                order.append(("transform", color))
            order += [("own", slot, color) for slot in WAVES[wave]]
            order += [("swap", slot, color) for slot in WAVES[wave]]
        for back in range(4):
            if 0 <= turn - back < len(turns):
                color, wave = turns[turn - back]
                order.append(("rows", WAVES[wave], color, back))
        for back in range(4):
            if 0 <= turn - back < len(turns):
                color, wave = turns[turn - back]
                if back == (2 if WAVES[wave][0] >= LATE else 3):
                    for (of, group), slots in left.items():
                        if of == color and slots and slots <= set(WAVES[wave]):
                            order.append(("product", color, group))
                        if of == color:
                            slots -= set(WAVES[wave])
    return order


def whole_kernel(
    table_ref, val_energy, cond_energy, sphere_ref, label_ref, psi_val, psi_cond, plane_ref, real_ref, imag_ref,
    val_all, cond_all, plane, val_rows, hit, place, high, low, sums, waves, picked, weight_ref, own_mask, got_mask,
    load_sem, out_sem, in_sem, part_sem, swap_sem, row_sem, send_sem, *chunks,
):
    wide = lax.axis_index("wide")
    x = lax.axis_index("narrow")
    z, y, core = wide // 8, wide // 2 % 4, wide % 2
    a = jnp.where(core == 0, y, z)
    b = jnp.where(core == 0, z, y)

    def at(da, db, other=0):
        aa, bb = (a + da) % 4, (b + db) % 4
        return jnp.where(core == 0, bb * 8 + aa * 2, aa * 8 + bb * 2 + 1)

    peers = {
        "a+": (at(1, 0), x),
        "a-": (at(3, 0), x),
        "b+": (at(0, 1), x),
        "b-": (at(0, 3), x),
        "swap": (wide + 1 - 2 * core, x),
        "x+": (wide, (x + 1) % 4),
        "x-": (wide, (x + 3) % 4),
    }
    def line(dz, dy):
        return ((z + dz) % 4 * 8 + (y + dy) % 4 * 2 + core, x)

    ring = [(wide, (x + d) % 4) for d in (1, 2, 3)]
    twin = wide + 1 - 2 * core
    near = ring + [(twin, x)] + [(twin, (x + d) % 4) for d in (1, 2, 3)]
    far = [line(dz, dy) for dz in range(4) for dy in range(4) if dz or dy]
    barrier = pltpu.get_barrier_semaphore()
    for peer in near + far:
        pl.semaphore_signal(barrier, inc=1, device_id=peer, device_id_type=MESH)
    loads = [
        pltpu.make_async_copy(source, target, load_sem.at[i])
        for i, (source, target) in enumerate(((psi_val, val_all), (psi_cond, cond_all), (plane_ref, plane)))
    ]
    for load in loads:
        load.start()

    band = lax.broadcasted_iota(jnp.int32, (128, 16), 0)
    there = jnp.max(jnp.where(band == table_ref[0:1, :], 1, 0), axis=1, keepdims=True)
    diagonal = lax.broadcasted_iota(jnp.int32, (128, 128), 0) == lax.broadcasted_iota(jnp.int32, (128, 128), 1)
    mask = jnp.broadcast_to(jnp.max(jnp.where(diagonal, there, 0), axis=0, keepdims=True), (8, 128))
    pl.semaphore_wait(barrier, len(near) + len(far))

    def work(step):
        def columns(tile, carry):
            columns_step(tile, label_ref, sphere_ref, x * 2048, hit, place)
            return carry

        lax.fori_loop(step * 4, step * 4 + 4, columns, 0)

    present = exchange(mask, (near, far), own_mask, got_mask, out_sem, in_sem, work)
    mine = deal(present, wide, val_energy[...], cond_energy[...], weight_ref)

    for load in loads:
        load.wait()
    pick_rows(val_all, mine, val_rows)

    held, rows = chunks[: len(COLORS)], chunks[len(COLORS) :]

    def steps_of(color):
        first, last = COLORS[color]

        def store(lane, real, imag):
            held[color][0, 0, 0 : last - first, pl.ds(lane, WIDTH)] = real
            held[color][1, 0, 0 : last - first, pl.ds(lane, WIDTH)] = imag

        return transform_steps(
            first, last - first, val_rows, cond_all, plane, hit, place, store, high, low, sums, waves, picked
        )

    sends = []

    def view(slot, color, part, which=0):
        size = SIZES[color]
        if part is None:
            return held[color].at[:, slot, which * size : (which + 1) * size, :]
        return held[color].at[part, slot, which * size : (which + 1) * size, :]

    def part_copy(slot, color, part, peer, target, send):
        return pltpu.make_async_remote_copy(
            src_ref=view(slot, color, part),
            dst_ref=view(target, color, part),
            send_sem=send_sem.at[send],
            recv_sem=part_sem.at[target, color, part if part is not None else 0],
            device_id=peers[peer],
            device_id_type=MESH,
        )

    def swap_copy(slot, color, send):
        return pltpu.make_async_remote_copy(
            src_ref=view(slot, color, None, 0),
            dst_ref=view(slot, color, None, 1),
            send_sem=send_sem.at[send],
            recv_sem=swap_sem.at[slot, color],
            device_id=peers["swap"],
            device_id_type=MESH,
        )

    def own_event(slot, color):
        if slot and in_halves(slot):
            part_copy(slot, color, 0, "a+", slot, 0).wait_recv()
            part_copy(slot, color, 1, "a+", slot, 0).wait_recv()
        elif slot:
            part_copy(slot, color, None, "a+", slot, 0).wait_recv()
        copies = [part_copy(slot, color, part, way, target, len(sends) + i) for i, (part, way, target) in enumerate(moves(slot))]
        copies.append(swap_copy(slot, color, len(sends) + len(copies)))
        for copy in copies:
            copy.start()
        sends.extend(copies)

    column = pl.multiple_of((y * 2 + core) * 256, 256)
    hops = ((x - z) % 4, (z - x) % 4)

    def row_copy(slot, color, which, way):
        size = SIZES[color]
        ref = rows[color].at[:, slot, which * size : (which + 1) * size, :]
        return pltpu.make_async_remote_copy(
            src_ref=ref,
            dst_ref=ref,
            send_sem=row_sem.at[1 + way, slot, color, which],
            recv_sem=row_sem.at[0, slot, color, which],
            device_id=peers["x+" if way == 0 else "x-"],
            device_id_type=MESH,
        )

    def row_ways(slot, which, hop):
        if slot < LATE:
            return [which] if hop < 3 else []
        return [0, 1] if hop == 0 else [which] if hop == 1 else []

    def row_events(slots, color, step):
        late = slots[0] >= LATE
        for which in range(2):
            for hop in ([step] if not late else [0] if step == 0 else [1, 3] if step == 1 else [2] if step == 2 else []):

                @pl.when(hops[which] == hop)
                def _():
                    at = slice(which * SIZES[color], (which + 1) * SIZES[color])
                    for slot in slots:
                        if hop == 0:
                            rows[color][:, slot, at, :] = held[color][:, slot, at, pl.ds(column, 256)]
                        else:
                            row_copy(slot, color, which, 0).wait_recv()
                        for way in row_ways(slot, which, hop):
                            row_copy(slot, color, which, way).start()

    width = 512

    def product(color, group, start):
        first, last = groups_of(SIZES[color])[group]
        depth = (last - first) * 2 * SIZES[color]
        weight = jnp.concatenate([weight_of(slot, color, which) for slot in range(first, last) for which in range(2)], axis=1)
        left = [(rows[color][part, first:last].reshape(depth, 256).astype(F32).T * weight).astype(BF) for part in range(2)]
        left_real = jnp.concatenate([left[0], left[1]], axis=0)
        left_imag = jnp.concatenate([left[1], -left[0]], axis=0)

        def tile(step, carry):
            at = pl.ds(pl.multiple_of(step * width, width), width)
            right = [held[color][part, first:last, :, at].reshape(depth, width) for part in range(2)]
            both = jnp.dot(left_real, right[0], preferred_element_type=F32)
            both = both + jnp.dot(left_imag, right[1], preferred_element_type=F32)
            return at, both

        def first_tile(step, carry):
            at, both = tile(step, carry)
            real_ref[:, at] = both[:256]
            imag_ref[:, at] = both[256:]
            return carry

        def later_tile(step, carry):
            at, both = tile(step, carry)
            real_ref[:, at] += both[:256]
            imag_ref[:, at] += both[256:]
            return carry

        lax.fori_loop(0, 2048 // width, first_tile if start else later_tile, 0)

    def weight_of(slot, color, which):
        da, db = ORDER[slot]
        device = at(da, db)
        if which:
            aa, bb = (b + da) % 4, (a + db) % 4
            device = jnp.where(core == 0, aa * 8 + bb * 2 + 1, bb * 8 + aa * 2)
        return weight_ref[pl.ds(device, 1), :][:, COLORS[color][0] : COLORS[color][1]]

    start = True
    for kind, *place_of in order_of_work():
        if kind == "transform":
            for step in steps_of(*place_of):
                step()
        elif kind == "own":
            own_event(*place_of)
        elif kind == "swap":
            swap_copy(*place_of, 0).wait_recv()
        elif kind == "rows":
            row_events(*place_of)
        else:
            product(*place_of, start)
            start = False

    for copy in sends:
        copy.wait_send()
    for which in range(2):
        for hop in range(3):

            @pl.when(hops[which] == hop)
            def _():
                for slot in range(16):
                    for color in range(len(COLORS)):
                        for way in row_ways(slot, which, hop):
                            row_copy(slot, color, which, way).wait_send()


def on_device(psi_val, psi_cond, energy_val, energy_cond, pair_table, sphere_map):
    vmem = pl.BlockSpec(memory_space=pltpu.VMEM)
    hbm = pl.BlockSpec(memory_space=pl.ANY)
    return pl.pallas_call(
        whole_kernel,
        out_shape=[jax.ShapeDtypeStruct((256, 2048), F32)] * 2,
        in_specs=[vmem] * 5 + [hbm] * 3,
        out_specs=[vmem] * 2,
        scratch_shapes=[
            pltpu.VMEM((128, FS**3), BF),
            pltpu.VMEM((NC, FS**3), BF),
            pltpu.VMEM((PLANE, 2 * HALF), BF),
            pltpu.VMEM((8, FS**3), F32),
            pltpu.VMEM((2 * HALF, 2048), BF),
            pltpu.VMEM((2, 2048), jnp.int32),
            pltpu.VMEM((KX * 2 * MOST, PLANE), BF),
            pltpu.VMEM((KX * 2 * MOST, PLANE), BF),
            pltpu.VMEM((KX * 2 * MOST, HALF), F32),
            pltpu.VMEM((KX * 2 * MOST, 2 * HALF), BF),
            pltpu.VMEM((KX * 2 * MOST, WIDTH), F32),
            pltpu.VMEM((32, 256), F32),
            pltpu.VMEM((3, 8, 128), jnp.int32),
            pltpu.VMEM((22, 8, 128), jnp.int32),
            pltpu.SemaphoreType.DMA((3,)),
            pltpu.SemaphoreType.DMA((22,)),
            pltpu.SemaphoreType.DMA((22,)),
            pltpu.SemaphoreType.DMA((16, len(COLORS), 2)),
            pltpu.SemaphoreType.DMA((16, len(COLORS))),
            pltpu.SemaphoreType.DMA((3, 16, len(COLORS), 2)),
            pltpu.SemaphoreType.DMA((48 * len(COLORS),)),
        ]
        + [pltpu.VMEM((2, 16, 2 * size, 2048), BF) for size in SIZES]
        + [pltpu.VMEM((2, 16, 2 * size, 256), BF) for size in SIZES],
        compiler_params=pltpu.CompilerParams(
            collective_id=0, has_side_effects=True, vmem_limit_bytes=58 * 2**20
        ),
        cost_estimate=pl.CostEstimate(flops=2 * 4096 * 512 * 2048, bytes_accessed=20 * 2**20, transcendentals=0),
        name="polarizability",
    )(
        pair_table.T,
        energy_val.reshape(1, -1),
        energy_cond.reshape(1, -1),
        sphere_map.reshape(1, -1),
        jnp.asarray(plane_labels()),
        psi_val,
        psi_cond,
        jnp.asarray(plane_table()).astype(BF),
    )


def solution(mesh):
    placed = (P(), P(), P(), P(), P(("wide", "narrow"), None), P())
    return jax.shard_map(
        on_device,
        mesh=mesh,
        in_specs=placed,
        out_specs=(P("wide", "narrow"), P("wide", "narrow")),
        check_vma=False,
    )
```

```python
import functools
import math

import jax
import jax.numpy as jnp
import numpy as np
from jax import lax
from jax.experimental import pallas as pl
from jax.experimental.pallas import tpu as pltpu
from jax.sharding import PartitionSpec as P

FS = 32
NC = 32
VB = 64
NG = 8192
PLANE = FS * FS
KX = 13
MESH = pl.DeviceIdType.MESH
BF = jnp.bfloat16
F32 = jnp.float32


def wrapped(index):
    return np.where(index >= FS // 2, index - FS, index)


def half_plane():
    index = np.arange(FS**3)
    length = wrapped(index // PLANE) ** 2 + wrapped(index // FS % FS) ** 2 + wrapped(index % FS) ** 2
    most = np.sort(length)[NG - 1]
    points = [
        (ky, kz)
        for ky in range(-15, 16)
        for kz in range(-15, 16)
        if ky * ky + kz * kz <= most and (ky > 0 or (ky == 0 and kz >= 0))
    ]
    points.sort(key=lambda point: (point[0] ** 2 + point[1] ** 2, point))
    return np.array(points)


POINTS = half_plane()
HALF = 256
TABLE_SCALE = 1.6211
TABLE_GAIN = 1.6245055860070914


NEAR = 128
FAR_KX = 9


def columns_of(first, second):
    return np.concatenate([first[:, :NEAR], second[:, :NEAR], first[:, NEAR:], second[:, NEAR:]], axis=1)


def plane_table():
    flat = np.arange(PLANE)
    phase = (flat // FS)[:, None] * POINTS[:, 0][None, :] + (flat % FS)[:, None] * POINTS[:, 1][None, :]
    angle = (phase % FS) * (2.0 * math.pi / FS)
    parts = []
    for wave in (np.cos(angle), np.sin(angle)):
        part = np.zeros((PLANE, HALF), np.float64)
        part[:, : len(POINTS)] = wave
        part[np.abs(part) < 1e-9] = 0.0
        parts.append(part)
    return (columns_of(*parts) * TABLE_SCALE).astype(np.float32)


def plane_labels():
    parts = np.full((2, HALF), -1, np.int32)
    for row, (ky, kz) in enumerate(POINTS):
        parts[0, row] = (ky % FS) * FS + kz % FS
        if (ky, kz) != (0, 0):
            parts[1, row] = (-ky % FS) * FS + (-kz) % FS
    return columns_of(parts[:1], parts[1:]).reshape(2 * HALF, 1)


def cosine(step):
    return math.cos(2.0 * math.pi * step / FS)


def combine(terms):
    total = None
    for factor, term in terms:
        if abs(factor) < 1e-12:
            continue
        if abs(abs(factor) - 1.0) < 1e-12:
            value = term
            if total is None:
                total = value if factor > 0 else -value
            else:
                total = total + value if factor > 0 else total - value
        else:
            value = term * factor
            total = value if total is None else total + value
    return total


def even_part(values, period, wanted):
    half = period // 2
    stride = FS // period
    out = {}
    odd = [k for k in wanted if k % 2]
    rest = [k for k in wanted if k % 2 == 0]
    if half == 1:
        for k in wanted:
            out[k] = values[0] + values[1] if k % 2 == 0 else values[0] - values[1]
        return out
    quarter = half // 2
    if odd:
        diff = [values[j] - values[half - j] for j in range(quarter)]
        for k in odd:
            out[k] = combine([(cosine(stride * j * k), diff[j]) for j in range(quarter)])
    if rest:
        folded = [values[j] + values[half - j] for j in range(quarter)] + [values[quarter]]
        inner = even_part(folded, half, [k // 2 for k in rest])
        for k in rest:
            out[k] = inner[k // 2]
    return out


def odd_part(values, period, wanted):
    half = period // 2
    stride = FS // period
    out = {}
    odd = [k for k in wanted if k % 2]
    rest = [k for k in wanted if k % 2 == 0]
    quarter = half // 2
    if odd:
        folded = [None] + [values[j] + values[half - j] for j in range(1, quarter)] + [values[quarter]]
        for k in odd:
            out[k] = combine(
                [(math.sin(2.0 * math.pi * stride * j * k / FS), folded[j]) for j in range(1, quarter + 1)]
            )
    if rest:
        live = [k for k in rest if k % half]
        if live:
            diff = [None] + [values[j] - values[half - j] for j in range(1, quarter)]
            inner = odd_part(diff, half, [k // 2 for k in live])
            for k in live:
                out[k] = inner[k // 2]
    return out


def exchange(mask, groups, own, got, out_sem, in_sem, work):
    own[0] = mask
    done, count = [], 0
    for step, group in enumerate(groups):
        copies = []
        for peer in group:
            copy = pltpu.make_async_remote_copy(
                src_ref=own.at[step],
                dst_ref=got.at[count],
                send_sem=out_sem.at[count],
                recv_sem=in_sem.at[count],
                device_id=peer,
                device_id_type=MESH,
            )
            copy.start()
            copies.append((copy, count))
            count += 1
        work(step)
        total = own[step]
        for copy, at in copies:
            copy.wait_recv()
            total = jnp.maximum(total, got[at])
        own[step + 1] = total
        done += copies
    for copy, _ in done:
        copy.wait_send()
    return own[len(groups)][0:1, :]


def deal(present, wide, val_energy, cond_energy, weight_ref):
    band = lax.broadcasted_iota(jnp.int32, (128, 128), 0)
    other = lax.broadcasted_iota(jnp.int32, (128, 128), 1)
    rank = jnp.sum(jnp.where(other < band, present, 0), axis=1, keepdims=True)
    across = jnp.sum(jnp.where(other == band, rank, 0), axis=0, keepdims=True)
    across = jnp.where(present > 0, across, -1)
    device = lax.broadcasted_iota(jnp.int32, (32, 128), 0)
    energy = [jnp.sum(jnp.where(across == 2 * device + i, val_energy, 0.0), axis=1, keepdims=True) for i in range(2)]
    lane = lax.broadcasted_iota(jnp.int32, (32, 256), 1)
    cond = jnp.concatenate([cond_energy] * 8, axis=1)
    gap = jnp.where(lane // NC % 2 == 0, energy[0], energy[1]) - cond
    weight_ref[...] = 2.0 / (gap * math.sqrt(VB * NC))
    row = lax.broadcasted_iota(jnp.int32, (8, 128), 0)
    return jnp.where((across == 2 * wide + row) & (row < 2), 1.0, 0.0)


def pick_rows(psi_ref, chosen, row_ref):
    left = chosen.astype(BF)

    def step(x, carry):
        at = pl.ds(pl.multiple_of(x * PLANE, PLANE), PLANE)
        row_ref[:, at] = jnp.dot(left, psi_ref[:, at], preferred_element_type=F32)
        return carry

    lax.fori_loop(0, FS, step, 0)


WIDTH = 256


def columns_step(tile, label_ref, sphere_ref, first_column, hit, place):
    lane = pl.multiple_of(tile * WIDTH, WIDTH)
    flat = sphere_ref[:, pl.ds(pl.multiple_of(first_column + lane, WIDTH), WIDTH)]
    kx = flat // PLANE
    ky = flat // FS % FS
    kz = flat % FS
    mirror = kx >= FS // 2
    ky = jnp.where(mirror, (FS - ky) % FS, ky)
    kz = jnp.where(mirror, (FS - kz) % FS, kz)
    place[0:1, pl.ds(lane, WIDTH)] = jnp.where(mirror, FS - kx, kx)
    place[1:2, pl.ds(lane, WIDTH)] = jnp.where(mirror, -1, 1)
    target = ky * FS + kz
    hit[:, pl.ds(lane, WIDTH)] = jnp.where(label_ref[...] == target, 1.0, 0.0).astype(BF)


def transform_steps(first, count, val_ref, cond_ref, table_ref, hit, place, store, high, low, sums, waves, picked):
    lanes = 128
    rows = 16
    pair = 2 * count
    middle = FAR_KX * pair
    every = KX * pair

    def x_block(block):
        part, cond_row = (first + block * rows) // NC, (first + block * rows) % NC

        def x_step(step, carry):
            lane = pl.multiple_of(step * lanes, lanes)
            density = []
            for x in range(FS):
                at = pl.ds(pl.multiple_of(x * PLANE + lane, lanes), lanes)
                density.append(cond_ref[cond_row : cond_row + rows, at].astype(F32) * val_ref[part : part + 1, at])
            even = [density[0]] + [density[j] + density[FS - j] for j in range(1, 16)] + [density[16]]
            odd = [None] + [density[j] - density[FS - j] for j in range(1, 16)]
            real = even_part(even, FS, list(range(KX)))
            imag = odd_part(odd, FS, list(range(KX)))
            for k in range(KX):
                for s, value in ((0, real[k]), (1, imag.get(k))):
                    at = k * pair + s * count + block * rows
                    if value is None:
                        value = jnp.zeros((rows, lanes), F32)
                    if s == 1:
                        value = -value
                    top = value.astype(BF)
                    high[at : at + rows, pl.ds(lane, lanes)] = top
                    low[at : at + rows, pl.ds(lane, lanes)] = (value - top.astype(F32)).astype(BF)
            return carry

        lax.fori_loop(0, PLANE // lanes, x_step, 0)

    def plane(side):
        live = every if side == 0 else middle
        table = table_ref[:, side * HALF : (side + 1) * HALF]
        both = jnp.dot(high[0:live, :], table, preferred_element_type=F32)
        sums[0:live, :] = both + jnp.dot(low[0:live, :], table, preferred_element_type=F32)
        scale = FS ** (-1.5) / TABLE_GAIN
        left, right = side * HALF, side * HALF + NEAR

        def combine_step(k, carry):
            at = pl.multiple_of(k * pair, pair)
            re = pl.ds(at, count)
            im = pl.ds(pl.multiple_of(at + count, count), count)
            re_cos, re_sin = sums[re, :NEAR] * scale, sums[re, NEAR:] * scale
            im_cos, im_sin = sums[im, :NEAR] * scale, sums[im, NEAR:] * scale
            waves[re, left : left + NEAR] = (re_cos + im_sin).astype(BF)
            waves[re, right : right + NEAR] = (re_cos - im_sin).astype(BF)
            waves[im, left : left + NEAR] = (im_cos - re_sin).astype(BF)
            waves[im, right : right + NEAR] = (im_cos + re_sin).astype(BF)
            return carry

        lax.fori_loop(0, KX if side == 0 else FAR_KX, combine_step, 0)

    def pick(tiles):
        def pick_step(tile, carry):
            lane = pl.multiple_of(tile * WIDTH, WIDTH)
            at = pl.ds(lane, WIDTH)
            picked[0:middle, :] = jnp.dot(waves[0:middle, :], hit[:, at], preferred_element_type=F32)
            picked[middle:every, :] = jnp.dot(waves[middle:every, :HALF], hit[:HALF, at], preferred_element_type=F32)
            kx = place[0:1, at]
            total = picked[0:pair, :]
            for k in range(1, KX):
                total = jnp.where(kx == k, picked[k * pair : (k + 1) * pair, :], total)
            sign = place[1:2, at].astype(F32)
            store(lane, total[:count].astype(BF), (total[count:] * sign).astype(BF))
            return carry

        lax.fori_loop(tiles[0], tiles[1], pick_step, 0)

    steps = [functools.partial(x_block, block) for block in range(count // rows)]
    steps += [functools.partial(plane, side) for side in range(2)]
    tiles = 2048 // WIDTH
    return steps + [functools.partial(pick, (i, i + tiles // 4)) for i in range(0, tiles, tiles // 4)]


ORDER = [
    (0, 0), (3, 0), (1, 0), (0, 3), (0, 1), (2, 0), (3, 3), (3, 1),
    (1, 3), (1, 1), (0, 2), (2, 3), (2, 1), (3, 2), (1, 2), (2, 2),
]
SLOT = {place: slot for slot, place in enumerate(ORDER)}
COLORS = [(0, 32), (32, 64)]
SIZES = [last - first for first, last in COLORS]
MOST = max(SIZES)
DEPTH = 512


def groups_of(size):
    count = max(1, DEPTH // (2 * size))
    return [(slot, min(slot + count, 16)) for slot in range(0, 16, count)]


def moves(slot):
    da, db = ORDER[slot]
    out = []
    if db == 0:
        if da == 0:
            out += [(None, "a+", SLOT[3, 0]), (None, "a-", SLOT[1, 0])]
        elif da == 3:
            out += [(0, "a+", SLOT[2, 0])]
        elif da == 1:
            out += [(1, "a-", SLOT[2, 0])]
        out += [(None, "b+", SLOT[da, 3]), (None, "b-", SLOT[da, 1])]
    elif db == 3:
        out += [(0, "b+", SLOT[da, 2])]
    elif db == 1:
        out += [(1, "b-", SLOT[da, 2])]
    return out


def in_halves(slot):
    da, db = ORDER[slot]
    return (da == 2 and db == 0) or db == 2


WAVES = [[0], [1, 2, 3, 4], [5, 6, 7], [8, 9, 10], [11, 12], [13, 14], [15]]
LATE = 11


def order_of_work():
    turns = [(color, wave) for wave in range(1, len(WAVES)) for color in range(len(COLORS))]
    turns = [(color, 0) for color in range(len(COLORS))] + turns
    order, left = [], {}
    for color, size in enumerate(SIZES):
        for group, (first, last) in enumerate(groups_of(size)):
            left[color, group] = {(slot, which) for slot in range(first, last) for which in range(2)}
    for turn in range(len(turns) + 5):
        if turn < len(turns):
            color, wave = turns[turn]
            if wave == 0:
                order.append(("transform", color))
            order += [("arrive", slot, color) for slot in WAVES[wave]]
        ripe = []
        for step in range(4):
            for before, (color, wave) in enumerate(turns):
                for which in range(2):
                    lag = step + (which if wave + 1 < len(WAVES) else 0)
                    if before + lag == turn:
                        if which and step == 0:
                            order += [("swap", slot, color) for slot in WAVES[wave]]
                        order.append(("rows", wave, color, which, step))
                        if step == (2 if WAVES[wave][0] >= LATE else 3):
                            ripe += [(color, slot, which) for slot in WAVES[wave]]
        if turn < len(turns):
            color, wave = turns[turn]
            order += [("push", slot, color) for slot in WAVES[wave]]
        for color, slot, which in ripe:
            for (of, group), slices in left.items():
                if of == color and (slot, which) in slices:
                    slices.remove((slot, which))
                    if not slices:
                        order.append(("product", color, group))
    return order


def whole_kernel(
    table_ref, val_energy, cond_energy, sphere_ref, label_ref, psi_val, psi_cond, plane_ref, real_ref, imag_ref,
    val_all, cond_all, plane, val_rows, hit, place, high, low, sums, waves, picked, weight_ref, own_mask, got_mask,
    load_sem, out_sem, in_sem, part_sem, swap_sem, row_sem, send_sem, *chunks,
):
    wide = lax.axis_index("wide")
    x = lax.axis_index("narrow")
    z, y, core = wide // 8, wide // 2 % 4, wide % 2
    a = jnp.where(core == 0, y, z)
    b = jnp.where(core == 0, z, y)

    def at(da, db, other=0):
        aa, bb = (a + da) % 4, (b + db) % 4
        return jnp.where(core == 0, bb * 8 + aa * 2, aa * 8 + bb * 2 + 1)

    peers = {
        "a+": (at(1, 0), x),
        "a-": (at(3, 0), x),
        "b+": (at(0, 1), x),
        "b-": (at(0, 3), x),
        "swap": (wide + 1 - 2 * core, x),
        "x+": (wide, (x + 1) % 4),
        "x-": (wide, (x + 3) % 4),
    }
    def line(dz, dy):
        return ((z + dz) % 4 * 8 + (y + dy) % 4 * 2 + core, x)

    ring = [(wide, (x + d) % 4) for d in (1, 2, 3)]
    twin = wide + 1 - 2 * core
    near = ring + [(twin, x)] + [(twin, (x + d) % 4) for d in (1, 2, 3)]
    far = [line(dz, dy) for dz in range(4) for dy in range(4) if dz or dy]
    barrier = pltpu.get_barrier_semaphore()
    for peer in near + far:
        pl.semaphore_signal(barrier, inc=1, device_id=peer, device_id_type=MESH)
    loads = [
        pltpu.make_async_copy(source, target, load_sem.at[i])
        for i, (source, target) in enumerate(((psi_val, val_all), (psi_cond, cond_all), (plane_ref, plane)))
    ]
    for load in loads:
        load.start()

    band = lax.broadcasted_iota(jnp.int32, (128, 16), 0)
    there = jnp.max(jnp.where(band == table_ref[0:1, :], 1, 0), axis=1, keepdims=True)
    diagonal = lax.broadcasted_iota(jnp.int32, (128, 128), 0) == lax.broadcasted_iota(jnp.int32, (128, 128), 1)
    mask = jnp.broadcast_to(jnp.max(jnp.where(diagonal, there, 0), axis=0, keepdims=True), (8, 128))
    pl.semaphore_wait(barrier, len(near) + len(far))

    def work(step):
        def columns(tile, carry):
            columns_step(tile, label_ref, sphere_ref, x * 2048, hit, place)
            return carry

        lax.fori_loop(step * 4, step * 4 + 4, columns, 0)

    present = exchange(mask, (near, far), own_mask, got_mask, out_sem, in_sem, work)
    mine = deal(present, wide, val_energy[...], cond_energy[...], weight_ref)

    for load in loads:
        load.wait()
    pick_rows(val_all, mine, val_rows)

    held, rows = chunks[: len(COLORS)], chunks[len(COLORS) :]

    def steps_of(color):
        first, last = COLORS[color]

        def store(lane, real, imag):
            held[color][0, 0, 0 : last - first, pl.ds(lane, WIDTH)] = real
            held[color][1, 0, 0 : last - first, pl.ds(lane, WIDTH)] = imag

        return transform_steps(
            first, last - first, val_rows, cond_all, plane, hit, place, store, high, low, sums, waves, picked
        )

    sends = []

    def view(slot, color, part, which=0):
        size = SIZES[color]
        if part is None:
            return held[color].at[:, slot, which * size : (which + 1) * size, :]
        return held[color].at[part, slot, which * size : (which + 1) * size, :]

    def part_copy(slot, color, part, peer, target, send):
        return pltpu.make_async_remote_copy(
            src_ref=view(slot, color, part),
            dst_ref=view(target, color, part),
            send_sem=send_sem.at[send],
            recv_sem=part_sem.at[target, color, part if part is not None else 0],
            device_id=peers[peer],
            device_id_type=MESH,
        )

    def swap_copy(slot, color, send):
        return pltpu.make_async_remote_copy(
            src_ref=view(slot, color, None, 0),
            dst_ref=view(slot, color, None, 1),
            send_sem=send_sem.at[send],
            recv_sem=swap_sem.at[slot, color],
            device_id=peers["swap"],
            device_id_type=MESH,
        )

    def arrive_event(slot, color):
        if slot and in_halves(slot):
            part_copy(slot, color, 0, "a+", slot, 0).wait_recv()
            part_copy(slot, color, 1, "a+", slot, 0).wait_recv()
        elif slot:
            part_copy(slot, color, None, "a+", slot, 0).wait_recv()
        copy = swap_copy(slot, color, len(sends))
        copy.start()
        sends.append(copy)

    def push_event(slot, color):
        for part, way, target in moves(slot):
            copy = part_copy(slot, color, part, way, target, len(sends))
            copy.start()
            sends.append(copy)

    column = pl.multiple_of((y * 2 + core) * 256, 256)
    hops = ((x - z) % 4, (z - x) % 4)

    def row_copy(wave, color, which, way):
        size = SIZES[color]
        slots = WAVES[wave]
        ref = rows[color].at[:, slots[0] : slots[-1] + 1, which * size : (which + 1) * size, :]
        return pltpu.make_async_remote_copy(
            src_ref=ref,
            dst_ref=ref,
            send_sem=row_sem.at[1 + way, wave, color, which],
            recv_sem=row_sem.at[0, wave, color, which],
            device_id=peers["x+" if way == 0 else "x-"],
            device_id_type=MESH,
        )

    def row_ways(wave, which, hop):
        if WAVES[wave][0] < LATE:
            return [which] if hop < 3 else []
        return [0, 1] if hop == 0 else [which] if hop == 1 else []

    def row_events(wave, color, which, step):
        late = WAVES[wave][0] >= LATE
        for hop in [step] if not late else [0] if step == 0 else [1, 3] if step == 1 else [2] if step == 2 else []:

            @pl.when(hops[which] == hop)
            def _():
                if hop == 0:
                    at = slice(which * SIZES[color], (which + 1) * SIZES[color])
                    for slot in WAVES[wave]:
                        rows[color][:, slot, at, :] = held[color][:, slot, at, pl.ds(column, 256)]
                else:
                    row_copy(wave, color, which, 0).wait_recv()
                for way in row_ways(wave, which, hop):
                    row_copy(wave, color, which, way).start()

    width = 512

    def product(color, group, start):
        first, last = groups_of(SIZES[color])[group]
        depth = (last - first) * 2 * SIZES[color]
        weight = jnp.concatenate([weight_of(slot, color, which) for slot in range(first, last) for which in range(2)], axis=1)
        left = [(rows[color][part, first:last].reshape(depth, 256).astype(F32).T * weight).astype(BF) for part in range(2)]
        left_real = jnp.concatenate([left[0], left[1]], axis=0)
        left_imag = jnp.concatenate([left[1], -left[0]], axis=0)

        def tile(step, carry):
            at = pl.ds(pl.multiple_of(step * width, width), width)
            right = [held[color][part, first:last, :, at].reshape(depth, width) for part in range(2)]
            both = jnp.dot(left_real, right[0], preferred_element_type=F32)
            both = both + jnp.dot(left_imag, right[1], preferred_element_type=F32)
            return at, both

        def first_tile(step, carry):
            at, both = tile(step, carry)
            real_ref[:, at] = both[:256]
            imag_ref[:, at] = both[256:]
            return carry

        def later_tile(step, carry):
            at, both = tile(step, carry)
            real_ref[:, at] += both[:256]
            imag_ref[:, at] += both[256:]
            return carry

        lax.fori_loop(0, 2048 // width, first_tile if start else later_tile, 0)

    def weight_of(slot, color, which):
        da, db = ORDER[slot]
        device = at(da, db)
        if which:
            aa, bb = (b + da) % 4, (a + db) % 4
            device = jnp.where(core == 0, aa * 8 + bb * 2 + 1, bb * 8 + aa * 2)
        return weight_ref[pl.ds(device, 1), :][:, COLORS[color][0] : COLORS[color][1]]

    start = True
    for kind, *place_of in order_of_work():
        if kind == "transform":
            for step in steps_of(*place_of):
                step()
        elif kind == "arrive":
            arrive_event(*place_of)
        elif kind == "push":
            push_event(*place_of)
        elif kind == "swap":
            swap_copy(*place_of, 0).wait_recv()
        elif kind == "rows":
            row_events(*place_of)
        else:
            product(*place_of, start)
            start = False

    for copy in sends:
        copy.wait_send()
    for which in range(2):
        for hop in range(3):

            @pl.when(hops[which] == hop)
            def _():
                for wave in range(len(WAVES)):
                    for color in range(len(COLORS)):
                        for way in row_ways(wave, which, hop):
                            row_copy(wave, color, which, way).wait_send()


def on_device(psi_val, psi_cond, energy_val, energy_cond, pair_table, sphere_map):
    vmem = pl.BlockSpec(memory_space=pltpu.VMEM)
    hbm = pl.BlockSpec(memory_space=pl.ANY)
    return pl.pallas_call(
        whole_kernel,
        out_shape=[jax.ShapeDtypeStruct((256, 2048), F32)] * 2,
        in_specs=[vmem] * 5 + [hbm] * 3,
        out_specs=[vmem] * 2,
        scratch_shapes=[
            pltpu.VMEM((128, FS**3), BF),
            pltpu.VMEM((NC, FS**3), BF),
            pltpu.VMEM((PLANE, 2 * HALF), BF),
            pltpu.VMEM((8, FS**3), F32),
            pltpu.VMEM((2 * HALF, 2048), BF),
            pltpu.VMEM((2, 2048), jnp.int32),
            pltpu.VMEM((KX * 2 * MOST, PLANE), BF),
            pltpu.VMEM((KX * 2 * MOST, PLANE), BF),
            pltpu.VMEM((KX * 2 * MOST, HALF), F32),
            pltpu.VMEM((KX * 2 * MOST, 2 * HALF), BF),
            pltpu.VMEM((KX * 2 * MOST, WIDTH), F32),
            pltpu.VMEM((32, 256), F32),
            pltpu.VMEM((3, 8, 128), jnp.int32),
            pltpu.VMEM((22, 8, 128), jnp.int32),
            pltpu.SemaphoreType.DMA((3,)),
            pltpu.SemaphoreType.DMA((22,)),
            pltpu.SemaphoreType.DMA((22,)),
            pltpu.SemaphoreType.DMA((16, len(COLORS), 2)),
            pltpu.SemaphoreType.DMA((16, len(COLORS))),
            pltpu.SemaphoreType.DMA((3, len(WAVES), len(COLORS), 2)),
            pltpu.SemaphoreType.DMA((48 * len(COLORS),)),
        ]
        + [pltpu.VMEM((2, 16, 2 * size, 2048), BF) for size in SIZES]
        + [pltpu.VMEM((2, 16, 2 * size, 256), BF) for size in SIZES],
        compiler_params=pltpu.CompilerParams(
            collective_id=0, has_side_effects=True, vmem_limit_bytes=58 * 2**20
        ),
        cost_estimate=pl.CostEstimate(flops=2 * 4096 * 512 * 2048, bytes_accessed=20 * 2**20, transcendentals=0),
        name="polarizability",
    )(
        pair_table.T,
        energy_val.reshape(1, -1),
        energy_cond.reshape(1, -1),
        sphere_map.reshape(1, -1),
        jnp.asarray(plane_labels()),
        psi_val,
        psi_cond,
        jnp.asarray(plane_table()).astype(BF),
    )


def solution(mesh):
    placed = (P(), P(), P(), P(), P(("wide", "narrow"), None), P())
    return jax.shard_map(
        on_device,
        mesh=mesh,
        in_specs=placed,
        out_specs=(P("wide", "narrow"), P("wide", "narrow")),
        check_vma=False,
    )
```

```python
import functools
import math

import jax
import jax.numpy as jnp
import numpy as np
from jax import lax
from jax.experimental import pallas as pl
from jax.experimental.pallas import tpu as pltpu
from jax.sharding import PartitionSpec as P

FS = 32
NC = 32
VB = 64
NG = 8192
PLANE = FS * FS
KX = 13
MESH = pl.DeviceIdType.MESH
BF = jnp.bfloat16
F32 = jnp.float32


def wrapped(index):
    return np.where(index >= FS // 2, index - FS, index)


def half_plane():
    index = np.arange(FS**3)
    length = wrapped(index // PLANE) ** 2 + wrapped(index // FS % FS) ** 2 + wrapped(index % FS) ** 2
    most = np.sort(length)[NG - 1]
    points = [
        (ky, kz)
        for ky in range(-15, 16)
        for kz in range(-15, 16)
        if ky * ky + kz * kz <= most and (ky > 0 or (ky == 0 and kz >= 0))
    ]
    points.sort(key=lambda point: (point[0] ** 2 + point[1] ** 2, point))
    return np.array(points)


POINTS = half_plane()
HALF = 256
TABLE_SCALE = 1.6211
TABLE_GAIN = 1.6245055860070914


NEAR = 128
FAR_KX = 9


def columns_of(first, second):
    return np.concatenate([first[:, :NEAR], second[:, :NEAR], first[:, NEAR:], second[:, NEAR:]], axis=1)


def plane_table():
    flat = np.arange(PLANE)
    phase = (flat // FS)[:, None] * POINTS[:, 0][None, :] + (flat % FS)[:, None] * POINTS[:, 1][None, :]
    angle = (phase % FS) * (2.0 * math.pi / FS)
    parts = []
    for wave in (np.cos(angle), np.sin(angle)):
        part = np.zeros((PLANE, HALF), np.float64)
        part[:, : len(POINTS)] = wave
        part[np.abs(part) < 1e-9] = 0.0
        parts.append(part)
    return (columns_of(*parts) * TABLE_SCALE).astype(np.float32)


def plane_labels():
    parts = np.full((2, HALF), -1, np.int32)
    for row, (ky, kz) in enumerate(POINTS):
        parts[0, row] = (ky % FS) * FS + kz % FS
        if (ky, kz) != (0, 0):
            parts[1, row] = (-ky % FS) * FS + (-kz) % FS
    return columns_of(parts[:1], parts[1:]).reshape(2 * HALF, 1)


def cosine(step):
    return math.cos(2.0 * math.pi * step / FS)


def combine(terms):
    total = None
    for factor, term in terms:
        if abs(factor) < 1e-12:
            continue
        if abs(abs(factor) - 1.0) < 1e-12:
            value = term
            if total is None:
                total = value if factor > 0 else -value
            else:
                total = total + value if factor > 0 else total - value
        else:
            value = term * factor
            total = value if total is None else total + value
    return total


def even_part(values, period, wanted):
    half = period // 2
    stride = FS // period
    out = {}
    odd = [k for k in wanted if k % 2]
    rest = [k for k in wanted if k % 2 == 0]
    if half == 1:
        for k in wanted:
            out[k] = values[0] + values[1] if k % 2 == 0 else values[0] - values[1]
        return out
    quarter = half // 2
    if odd:
        diff = [values[j] - values[half - j] for j in range(quarter)]
        for k in odd:
            out[k] = combine([(cosine(stride * j * k), diff[j]) for j in range(quarter)])
    if rest:
        folded = [values[j] + values[half - j] for j in range(quarter)] + [values[quarter]]
        inner = even_part(folded, half, [k // 2 for k in rest])
        for k in rest:
            out[k] = inner[k // 2]
    return out


def odd_part(values, period, wanted):
    half = period // 2
    stride = FS // period
    out = {}
    odd = [k for k in wanted if k % 2]
    rest = [k for k in wanted if k % 2 == 0]
    quarter = half // 2
    if odd:
        folded = [None] + [values[j] + values[half - j] for j in range(1, quarter)] + [values[quarter]]
        for k in odd:
            out[k] = combine(
                [(math.sin(2.0 * math.pi * stride * j * k / FS), folded[j]) for j in range(1, quarter + 1)]
            )
    if rest:
        live = [k for k in rest if k % half]
        if live:
            diff = [None] + [values[j] - values[half - j] for j in range(1, quarter)]
            inner = odd_part(diff, half, [k // 2 for k in live])
            for k in live:
                out[k] = inner[k // 2]
    return out


def exchange(mask, groups, own, got, out_sem, in_sem, work):
    own[0] = mask
    done, count = [], 0
    for step, group in enumerate(groups):
        copies = []
        for peer in group:
            copy = pltpu.make_async_remote_copy(
                src_ref=own.at[step],
                dst_ref=got.at[count],
                send_sem=out_sem.at[count],
                recv_sem=in_sem.at[count],
                device_id=peer,
                device_id_type=MESH,
            )
            copy.start()
            copies.append((copy, count))
            count += 1
        work(step)
        total = own[step]
        for copy, at in copies:
            copy.wait_recv()
            total = jnp.maximum(total, got[at])
        own[step + 1] = total
        done += copies
    for copy, _ in done:
        copy.wait_send()
    return own[len(groups)][0:1, :]


def deal(present, wide, val_energy, cond_energy, weight_ref):
    band = lax.broadcasted_iota(jnp.int32, (128, 128), 0)
    other = lax.broadcasted_iota(jnp.int32, (128, 128), 1)
    rank = jnp.sum(jnp.where(other < band, present, 0), axis=1, keepdims=True)
    across = jnp.sum(jnp.where(other == band, rank, 0), axis=0, keepdims=True)
    across = jnp.where(present > 0, across, -1)
    device = lax.broadcasted_iota(jnp.int32, (32, 128), 0)
    energy = [jnp.sum(jnp.where(across == 2 * device + i, val_energy, 0.0), axis=1, keepdims=True) for i in range(2)]
    lane = lax.broadcasted_iota(jnp.int32, (32, 256), 1)
    cond = jnp.concatenate([cond_energy] * 8, axis=1)
    gap = jnp.where(lane // NC % 2 == 0, energy[0], energy[1]) - cond
    weight_ref[...] = 2.0 / (gap * math.sqrt(VB * NC))
    row = lax.broadcasted_iota(jnp.int32, (8, 128), 0)
    return jnp.where((across == 2 * wide + row) & (row < 2), 1.0, 0.0)


WIDTH = 256


def columns_step(tile, label_ref, sphere_ref, first_column, hit, place):
    lane = pl.multiple_of(tile * WIDTH, WIDTH)
    flat = sphere_ref[:, pl.ds(pl.multiple_of(first_column + lane, WIDTH), WIDTH)]
    kx = flat // PLANE
    ky = flat // FS % FS
    kz = flat % FS
    mirror = kx >= FS // 2
    ky = jnp.where(mirror, (FS - ky) % FS, ky)
    kz = jnp.where(mirror, (FS - kz) % FS, kz)
    place[0:1, pl.ds(lane, WIDTH)] = jnp.where(mirror, FS - kx, kx)
    place[1:2, pl.ds(lane, WIDTH)] = jnp.where(mirror, -1, 1)
    target = ky * FS + kz
    hit[:, pl.ds(lane, WIDTH)] = jnp.where(label_ref[...] == target, 1.0, 0.0).astype(BF)


def transform_steps(first, count, chosen, psi_ref, val_ref, cond_ref, table_ref, hit, place, store, high, low, sums, waves, picked):
    lanes = 128
    rows = 16
    pair = 2 * count
    middle = FAR_KX * pair
    every = KX * pair

    def rows_at(step):
        for x in range(FS):
            at = pl.ds(pl.multiple_of(x * PLANE + step * lanes, lanes), lanes)
            val_ref[:, at] = jnp.dot(chosen.astype(BF), psi_ref[:, at], preferred_element_type=F32)

    def x_step(step, carry):
        lane = pl.multiple_of(step * lanes, lanes)
        if chosen is not None:
            rows_at(step)
        for block in range(count // rows):
            part, cond_row = (first + block * rows) // NC, (first + block * rows) % NC
            density = []
            for x in range(FS):
                at = pl.ds(pl.multiple_of(x * PLANE + lane, lanes), lanes)
                density.append(cond_ref[cond_row : cond_row + rows, at].astype(F32) * val_ref[part : part + 1, at])
            even = [density[0]] + [density[j] + density[FS - j] for j in range(1, 16)] + [density[16]]
            odd = [None] + [density[j] - density[FS - j] for j in range(1, 16)]
            real = even_part(even, FS, list(range(KX)))
            imag = odd_part(odd, FS, list(range(KX)))
            for k in range(KX):
                for s, value in ((0, real[k]), (1, imag.get(k))):
                    at = k * pair + s * count + block * rows
                    if value is None:
                        value = jnp.zeros((rows, lanes), F32)
                    if s == 1:
                        value = -value
                    top = value.astype(BF)
                    high[at : at + rows, pl.ds(lane, lanes)] = top
                    low[at : at + rows, pl.ds(lane, lanes)] = (value - top.astype(F32)).astype(BF)
        return carry

    def x_all():
        lax.fori_loop(0, PLANE // lanes, x_step, 0)

    def plane(side):
        live = every if side == 0 else middle
        table = table_ref[:, side * HALF : (side + 1) * HALF]
        both = jnp.dot(high[0:live, :], table, preferred_element_type=F32)
        sums[0:live, :] = both + jnp.dot(low[0:live, :], table, preferred_element_type=F32)
        scale = FS ** (-1.5) / TABLE_GAIN
        left, right = side * HALF, side * HALF + NEAR

        def combine_step(k, carry):
            at = pl.multiple_of(k * pair, pair)
            re = pl.ds(at, count)
            im = pl.ds(pl.multiple_of(at + count, count), count)
            re_cos, re_sin = sums[re, :NEAR] * scale, sums[re, NEAR:] * scale
            im_cos, im_sin = sums[im, :NEAR] * scale, sums[im, NEAR:] * scale
            waves[re, left : left + NEAR] = (re_cos + im_sin).astype(BF)
            waves[re, right : right + NEAR] = (re_cos - im_sin).astype(BF)
            waves[im, left : left + NEAR] = (im_cos - re_sin).astype(BF)
            waves[im, right : right + NEAR] = (im_cos + re_sin).astype(BF)
            return carry

        lax.fori_loop(0, KX if side == 0 else FAR_KX, combine_step, 0)

    def pick(tiles):
        def pick_step(tile, carry):
            lane = pl.multiple_of(tile * WIDTH, WIDTH)
            at = pl.ds(lane, WIDTH)
            picked[0:middle, :] = jnp.dot(waves[0:middle, :], hit[:, at], preferred_element_type=F32)
            picked[middle:every, :] = jnp.dot(waves[middle:every, :HALF], hit[:HALF, at], preferred_element_type=F32)
            kx = place[0:1, at]
            total = picked[0:pair, :]
            for k in range(1, KX):
                total = jnp.where(kx == k, picked[k * pair : (k + 1) * pair, :], total)
            sign = place[1:2, at].astype(F32)
            store(lane, total[:count].astype(BF), (total[count:] * sign).astype(BF))
            return carry

        lax.fori_loop(tiles[0], tiles[1], pick_step, 0)

    steps = [x_all] + [functools.partial(plane, side) for side in range(2)]
    tiles = 2048 // WIDTH
    return steps + [functools.partial(pick, (i, i + tiles // 4)) for i in range(0, tiles, tiles // 4)]


ORDER = [
    (0, 0), (3, 0), (1, 0), (0, 3), (0, 1), (2, 0), (3, 3), (3, 1),
    (1, 3), (1, 1), (0, 2), (2, 3), (2, 1), (3, 2), (1, 2), (2, 2),
]
SLOT = {place: slot for slot, place in enumerate(ORDER)}
COLORS = [(0, 32), (32, 64)]
SIZES = [last - first for first, last in COLORS]
MOST = max(SIZES)
DEPTH = 512


def groups_of(size):
    count = max(1, DEPTH // (2 * size))
    return [(slot, min(slot + count, 16)) for slot in range(0, 16, count)]


def moves(slot):
    da, db = ORDER[slot]
    out = []
    if db == 0:
        if da == 0:
            out += [(None, "a+", SLOT[3, 0]), (None, "a-", SLOT[1, 0])]
        elif da == 3:
            out += [(0, "a+", SLOT[2, 0])]
        elif da == 1:
            out += [(1, "a-", SLOT[2, 0])]
        out += [(None, "b+", SLOT[da, 3]), (None, "b-", SLOT[da, 1])]
    elif db == 3:
        out += [(0, "b+", SLOT[da, 2])]
    elif db == 1:
        out += [(1, "b-", SLOT[da, 2])]
    return out


def in_halves(slot):
    da, db = ORDER[slot]
    return (da == 2 and db == 0) or db == 2


WAVES = [[0], [1, 2, 3, 4], [5, 6, 7], [8, 9, 10], [11, 12], [13, 14], [15]]
LATE = 11


def order_of_work():
    turns = [(color, wave) for wave in range(1, len(WAVES)) for color in range(len(COLORS))]
    turns = [(color, 0) for color in range(len(COLORS))] + turns
    order, left = [], {}
    for color, size in enumerate(SIZES):
        for group, (first, last) in enumerate(groups_of(size)):
            left[color, group] = {(slot, which) for slot in range(first, last) for which in range(2)}
    for turn in range(len(turns) + 5):
        if turn < len(turns):
            color, wave = turns[turn]
            if wave == 0:
                order.append(("transform", color))
            order += [("arrive", slot, color) for slot in WAVES[wave]]
        ripe = []
        for step in range(4):
            for before, (color, wave) in enumerate(turns):
                for which in range(2):
                    lag = step + (which if wave + 1 < len(WAVES) else 0)
                    if before + lag == turn:
                        if which and step == 0:
                            order += [("swap", slot, color) for slot in WAVES[wave]]
                        order.append(("rows", wave, color, which, step))
                        if step == (2 if WAVES[wave][0] >= LATE else 3):
                            ripe += [(color, slot, which) for slot in WAVES[wave]]
        if turn < len(turns):
            color, wave = turns[turn]
            order += [("push", slot, color) for slot in WAVES[wave]]
        for color, slot, which in ripe:
            for (of, group), slices in left.items():
                if of == color and (slot, which) in slices:
                    slices.remove((slot, which))
                    if not slices:
                        order.append(("product", color, group))
    return order


def whole_kernel(
    table_ref, val_energy, cond_energy, sphere_ref, label_ref, psi_val, psi_cond, plane_ref, real_ref, imag_ref,
    val_all, cond_all, plane, val_rows, hit, place, high, low, sums, waves, picked, weight_ref, own_mask, got_mask,
    load_sem, out_sem, in_sem, part_sem, swap_sem, row_sem, send_sem, *chunks,
):
    wide = lax.axis_index("wide")
    x = lax.axis_index("narrow")
    z, y, core = wide // 8, wide // 2 % 4, wide % 2
    a = jnp.where(core == 0, y, z)
    b = jnp.where(core == 0, z, y)

    def at(da, db, other=0):
        aa, bb = (a + da) % 4, (b + db) % 4
        return jnp.where(core == 0, bb * 8 + aa * 2, aa * 8 + bb * 2 + 1)

    peers = {
        "a+": (at(1, 0), x),
        "a-": (at(3, 0), x),
        "b+": (at(0, 1), x),
        "b-": (at(0, 3), x),
        "swap": (wide + 1 - 2 * core, x),
        "x+": (wide, (x + 1) % 4),
        "x-": (wide, (x + 3) % 4),
    }
    def line(dz, dy):
        return ((z + dz) % 4 * 8 + (y + dy) % 4 * 2 + core, x)

    ring = [(wide, (x + d) % 4) for d in (1, 2, 3)]
    twin = wide + 1 - 2 * core
    near = ring + [(twin, x)] + [(twin, (x + d) % 4) for d in (1, 2, 3)]
    far = [line(dz, dy) for dz in range(4) for dy in range(4) if dz or dy]
    barrier = pltpu.get_barrier_semaphore()
    for peer in near + far:
        pl.semaphore_signal(barrier, inc=1, device_id=peer, device_id_type=MESH)
    loads = [
        pltpu.make_async_copy(source, target, load_sem.at[i])
        for i, (source, target) in enumerate(((psi_val, val_all), (psi_cond, cond_all), (plane_ref, plane)))
    ]
    for load in loads:
        load.start()

    band = lax.broadcasted_iota(jnp.int32, (128, 16), 0)
    there = jnp.max(jnp.where(band == table_ref[0:1, :], 1, 0), axis=1, keepdims=True)
    diagonal = lax.broadcasted_iota(jnp.int32, (128, 128), 0) == lax.broadcasted_iota(jnp.int32, (128, 128), 1)
    mask = jnp.broadcast_to(jnp.max(jnp.where(diagonal, there, 0), axis=0, keepdims=True), (8, 128))
    pl.semaphore_wait(barrier, len(near) + len(far))

    def work(step):
        def columns(tile, carry):
            columns_step(tile, label_ref, sphere_ref, x * 2048, hit, place)
            return carry

        lax.fori_loop(step * 4, step * 4 + 4, columns, 0)

    present = exchange(mask, (near, far), own_mask, got_mask, out_sem, in_sem, work)
    mine = deal(present, wide, val_energy[...], cond_energy[...], weight_ref)

    for load in loads:
        load.wait()

    held, rows = chunks[: len(COLORS)], chunks[len(COLORS) :]

    def steps_of(color):
        first, last = COLORS[color]

        def store(lane, real, imag):
            held[color][0, 0, 0 : last - first, pl.ds(lane, WIDTH)] = real
            held[color][1, 0, 0 : last - first, pl.ds(lane, WIDTH)] = imag

        return transform_steps(
            first, last - first, mine if color == 0 else None, val_all, val_rows, cond_all, plane, hit, place, store, high, low, sums, waves, picked
        )

    sends = []

    def view(slot, color, part, which=0):
        size = SIZES[color]
        if part is None:
            return held[color].at[:, slot, which * size : (which + 1) * size, :]
        return held[color].at[part, slot, which * size : (which + 1) * size, :]

    def part_copy(slot, color, part, peer, target, send):
        return pltpu.make_async_remote_copy(
            src_ref=view(slot, color, part),
            dst_ref=view(target, color, part),
            send_sem=send_sem.at[send],
            recv_sem=part_sem.at[target, color, part if part is not None else 0],
            device_id=peers[peer],
            device_id_type=MESH,
        )

    def swap_copy(slot, color, send):
        return pltpu.make_async_remote_copy(
            src_ref=view(slot, color, None, 0),
            dst_ref=view(slot, color, None, 1),
            send_sem=send_sem.at[send],
            recv_sem=swap_sem.at[slot, color],
            device_id=peers["swap"],
            device_id_type=MESH,
        )

    def arrive_event(slot, color):
        if slot and in_halves(slot):
            part_copy(slot, color, 0, "a+", slot, 0).wait_recv()
            part_copy(slot, color, 1, "a+", slot, 0).wait_recv()
        elif slot:
            part_copy(slot, color, None, "a+", slot, 0).wait_recv()
        copy = swap_copy(slot, color, len(sends))
        copy.start()
        sends.append(copy)

    def push_event(slot, color):
        for part, way, target in moves(slot):
            copy = part_copy(slot, color, part, way, target, len(sends))
            copy.start()
            sends.append(copy)

    column = pl.multiple_of((y * 2 + core) * 256, 256)
    hops = ((x - z) % 4, (z - x) % 4)

    def row_copy(wave, color, which, way):
        size = SIZES[color]
        slots = WAVES[wave]
        ref = rows[color].at[:, slots[0] : slots[-1] + 1, which * size : (which + 1) * size, :]
        return pltpu.make_async_remote_copy(
            src_ref=ref,
            dst_ref=ref,
            send_sem=row_sem.at[1 + way, wave, color, which],
            recv_sem=row_sem.at[0, wave, color, which],
            device_id=peers["x+" if way == 0 else "x-"],
            device_id_type=MESH,
        )

    def row_ways(wave, which, hop):
        if WAVES[wave][0] < LATE:
            return [which] if hop < 3 else []
        return [0, 1] if hop == 0 else [which] if hop == 1 else []

    def row_events(wave, color, which, step):
        late = WAVES[wave][0] >= LATE
        for hop in [step] if not late else [0] if step == 0 else [1, 3] if step == 1 else [2] if step == 2 else []:

            @pl.when(hops[which] == hop)
            def _():
                if hop == 0:
                    at = slice(which * SIZES[color], (which + 1) * SIZES[color])
                    for slot in WAVES[wave]:
                        rows[color][:, slot, at, :] = held[color][:, slot, at, pl.ds(column, 256)]
                else:
                    row_copy(wave, color, which, 0).wait_recv()
                for way in row_ways(wave, which, hop):
                    row_copy(wave, color, which, way).start()

    width = 512

    def product(color, group, start):
        first, last = groups_of(SIZES[color])[group]
        depth = (last - first) * 2 * SIZES[color]
        weight = jnp.concatenate([weight_of(slot, color, which) for slot in range(first, last) for which in range(2)], axis=1)
        left = [(rows[color][part, first:last].reshape(depth, 256).astype(F32).T * weight).astype(BF) for part in range(2)]
        left_real = jnp.concatenate([left[0], left[1]], axis=0)
        left_imag = jnp.concatenate([left[1], -left[0]], axis=0)

        def tile(step, carry):
            at = pl.ds(pl.multiple_of(step * width, width), width)
            right = [held[color][part, first:last, :, at].reshape(depth, width) for part in range(2)]
            both = jnp.dot(left_real, right[0], preferred_element_type=F32)
            both = both + jnp.dot(left_imag, right[1], preferred_element_type=F32)
            return at, both

        def first_tile(step, carry):
            at, both = tile(step, carry)
            real_ref[:, at] = both[:256]
            imag_ref[:, at] = both[256:]
            return carry

        def later_tile(step, carry):
            at, both = tile(step, carry)
            real_ref[:, at] += both[:256]
            imag_ref[:, at] += both[256:]
            return carry

        lax.fori_loop(0, 2048 // width, first_tile if start else later_tile, 0)

    def weight_of(slot, color, which):
        da, db = ORDER[slot]
        device = at(da, db)
        if which:
            aa, bb = (b + da) % 4, (a + db) % 4
            device = jnp.where(core == 0, aa * 8 + bb * 2 + 1, bb * 8 + aa * 2)
        return weight_ref[pl.ds(device, 1), :][:, COLORS[color][0] : COLORS[color][1]]

    start = True
    for kind, *place_of in order_of_work():
        if kind == "transform":
            for step in steps_of(*place_of):
                step()
        elif kind == "arrive":
            arrive_event(*place_of)
        elif kind == "push":
            push_event(*place_of)
        elif kind == "swap":
            swap_copy(*place_of, 0).wait_recv()
        elif kind == "rows":
            row_events(*place_of)
        else:
            product(*place_of, start)
            start = False

    for copy in sends:
        copy.wait_send()
    for which in range(2):
        for hop in range(3):

            @pl.when(hops[which] == hop)
            def _():
                for wave in range(len(WAVES)):
                    for color in range(len(COLORS)):
                        for way in row_ways(wave, which, hop):
                            row_copy(wave, color, which, way).wait_send()


def on_device(psi_val, psi_cond, energy_val, energy_cond, pair_table, sphere_map):
    vmem = pl.BlockSpec(memory_space=pltpu.VMEM)
    hbm = pl.BlockSpec(memory_space=pl.ANY)
    return pl.pallas_call(
        whole_kernel,
        out_shape=[jax.ShapeDtypeStruct((256, 2048), F32)] * 2,
        in_specs=[vmem] * 5 + [hbm] * 3,
        out_specs=[vmem] * 2,
        scratch_shapes=[
            pltpu.VMEM((128, FS**3), BF),
            pltpu.VMEM((NC, FS**3), BF),
            pltpu.VMEM((PLANE, 2 * HALF), BF),
            pltpu.VMEM((8, FS**3), F32),
            pltpu.VMEM((2 * HALF, 2048), BF),
            pltpu.VMEM((2, 2048), jnp.int32),
            pltpu.VMEM((KX * 2 * MOST, PLANE), BF),
            pltpu.VMEM((KX * 2 * MOST, PLANE), BF),
            pltpu.VMEM((KX * 2 * MOST, HALF), F32),
            pltpu.VMEM((KX * 2 * MOST, 2 * HALF), BF),
            pltpu.VMEM((KX * 2 * MOST, WIDTH), F32),
            pltpu.VMEM((32, 256), F32),
            pltpu.VMEM((3, 8, 128), jnp.int32),
            pltpu.VMEM((22, 8, 128), jnp.int32),
            pltpu.SemaphoreType.DMA((3,)),
            pltpu.SemaphoreType.DMA((22,)),
            pltpu.SemaphoreType.DMA((22,)),
            pltpu.SemaphoreType.DMA((16, len(COLORS), 2)),
            pltpu.SemaphoreType.DMA((16, len(COLORS))),
            pltpu.SemaphoreType.DMA((3, len(WAVES), len(COLORS), 2)),
            pltpu.SemaphoreType.DMA((48 * len(COLORS),)),
        ]
        + [pltpu.VMEM((2, 16, 2 * size, 2048), BF) for size in SIZES]
        + [pltpu.VMEM((2, 16, 2 * size, 256), BF) for size in SIZES],
        compiler_params=pltpu.CompilerParams(
            collective_id=0, has_side_effects=True, vmem_limit_bytes=58 * 2**20
        ),
        cost_estimate=pl.CostEstimate(flops=2 * 4096 * 512 * 2048, bytes_accessed=20 * 2**20, transcendentals=0),
        name="polarizability",
    )(
        pair_table.T,
        energy_val.reshape(1, -1),
        energy_cond.reshape(1, -1),
        sphere_map.reshape(1, -1),
        jnp.asarray(plane_labels()),
        psi_val,
        psi_cond,
        jnp.asarray(plane_table()).astype(BF),
    )


def solution(mesh):
    placed = (P(), P(), P(), P(), P(("wide", "narrow"), None), P())
    return jax.shard_map(
        on_device,
        mesh=mesh,
        in_specs=placed,
        out_specs=(P("wide", "narrow"), P("wide", "narrow")),
        check_vma=False,
    )
```
